32 devices in a mesh: row: 4 (over y, core), col: 8 (over z, x).
Axes of the slice: x: 2, y: 2, z: 4, core: 2. Of those that a mesh axis runs over, the one named last changes fastest.
Arguments:
- scores: float32 [32, 24576], P(None, ('row', 'col')), may hold values from -60 to 60
- tile_values: bfloat16 [4, 8, 240, 128, 128], P('row', 'col'), may hold values from 0 to 1
- tile_rows: int32 [4, 8, 240], P('row', 'col'), may hold values from 0 to 47, as said below
- tile_cols: int32 [4, 8, 240], P('row', 'col'), may hold values from 0 to 23, as said below
- tile_count: int32 [4, 8], P('row', 'col'), may hold values from 120 to 240, as said below
Outputs:
- solution: float32 [32, 24576], P(None, ('row', 'col'))
- residual: float32 [32, 24576], P(None, ('row', 'col'))
The draws below stay inside these ranges and needn't reach their ends.
Inputs may be any that keep to these rules, and one draw needn't show every extreme that they name: `tile_rows`: on every device each local row tile is named by exactly 5 of the 240 slots. `tile_cols`: on every device each local column tile is named by exactly 10 of the slots. Only the first tile_count slots of a device are live; some device has all 240 slots live.
All inputs are finite; a program needn't handle non-finite values.
Results may differ from the reference program's by a relative error of at most 0.0031.
Values may be sent and summed in bfloat16 or wider, within the bound.
No kernel may reach another device: no remote copies, remote signals or barrier semaphores. Data moves between devices by JAX's collectives and lax.ppermute only.
A program may use at most 128 MiB of HBM per device.

```python
import math
import jax
import jax.numpy as jnp
from jax import lax

TASKS = 32
TILE = 128
PER_ROW = 5
TPB = 6
ITERS = 3
DOCS = 24576
ROW_TILES = 48
COL_TILES = 24
SLOTS = 240
N_ROW = 4
N_COL = 8


def tile_lists(key):
    device_keys = jax.random.split(jax.random.fold_in(key, 11), N_ROW * N_COL)

    def one_device(device_key):
        first_key, second_key = jax.random.split(device_key)
        row_ids = jax.random.permutation(first_key, SLOTS) % ROW_TILES
        col_ids = jax.random.permutation(second_key, SLOTS) % COL_TILES
        return (row_ids.astype(jnp.int32), col_ids.astype(jnp.int32))
    row_ids, col_ids = jax.vmap(one_device)(device_keys)
    return (row_ids.reshape(N_ROW, N_COL, SLOTS), col_ids.reshape(N_ROW, N_COL, SLOTS))


def draw_tile_rows(key, part):
    return tile_lists(key)[0]


def draw_tile_cols(key, part):
    return tile_lists(key)[1]


def draw_tile_count(key, part):
    counts = jax.random.randint(jax.random.fold_in(key, 23), (N_ROW * N_COL,), SLOTS // 2, SLOTS + 1)
    full_device = jax.random.randint(jax.random.fold_in(key, 29), (), 0, N_ROW * N_COL)
    counts = counts.at[full_device].set(SLOTS)
    return counts.astype(jnp.int32).reshape(N_ROW, N_COL)


def draw_tile_values(key, part):
    density = 16.0 / (PER_ROW * N_COL * TILE)
    uniform_part = jax.random.uniform(jax.random.fold_in(key, 37), (N_ROW, N_COL, SLOTS, TILE, TILE), jnp.float32)
    lowest = 0.25
    weights = lowest + (1.0 - lowest) * (uniform_part / density)
    chosen = jnp.where(uniform_part < density, weights, 0.0)
    return chosen.astype(jnp.bfloat16)


def draw_scores(key, part):
    first_key, second_key = jax.random.split(jax.random.fold_in(key, 5))
    task_scale = jnp.exp(jax.random.uniform(first_key, (TASKS, 1), jnp.float32, math.log(0.3), math.log(3.0)))
    doc_scale = jnp.exp(math.log(3.0) * jnp.arange(DOCS, dtype=jnp.float32) / (DOCS - 1))[None, :]
    base_values = jnp.clip(jax.random.normal(second_key, (TASKS, DOCS), jnp.float32), -6.0, 6.0)
    return (base_values * task_scale * doc_scale).astype(jnp.float32)


def setup_inputs(seed: int = 0) -> dict:
    arg_keys = jax.random.split(jax.random.key(seed), 6)
    return {
        "scores": draw_scores(jax.random.fold_in(arg_keys[5], 71), 0),
        "tile_values": draw_tile_values(jax.random.fold_in(arg_keys[5], 71), 0),
        "tile_rows": draw_tile_rows(jax.random.fold_in(arg_keys[5], 71), 0),
        "tile_cols": draw_tile_cols(jax.random.fold_in(arg_keys[5], 71), 0),
        "tile_count": draw_tile_count(jax.random.fold_in(arg_keys[5], 71), 0),
    }


coupling = 0.2


def tile_products(field, tile_values, tile_rows, tile_cols, tile_count):
    field_rows = field.shape[0]
    blocks = field.astype(jnp.bfloat16).reshape(field_rows, DOCS // TILE, TILE)
    dev_tiles = tile_values.reshape(N_ROW * N_COL, SLOTS, TILE, TILE)
    local_rows = tile_rows.reshape(N_ROW * N_COL, SLOTS)
    local_cols = tile_cols.reshape(N_ROW * N_COL, SLOTS)
    live_counts = tile_count.reshape(N_ROW * N_COL)
    device_ids = jnp.arange(N_ROW * N_COL, dtype=jnp.int32)

    def one_device(running, device_item):
        forward_sum, backward_sum = running
        tiles_here, rows_here, cols_here, live_count, device_id = device_item
        row_block = device_id // N_COL
        col_block = device_id % N_COL
        global_rows = (row_block * ROW_TILES + rows_here).astype(jnp.int32)
        global_cols = (((cols_here // TPB) * N_COL + col_block) * TPB + cols_here % TPB).astype(jnp.int32)
        live_mask = (jnp.arange(SLOTS, dtype=jnp.int32) < live_count).astype(jnp.float32)
        wide_tiles = tiles_here.astype(jnp.float32)
        col_pieces = jnp.take(blocks, global_cols, axis=1).astype(jnp.float32)
        row_pieces = jnp.take(blocks, global_rows, axis=1).astype(jnp.float32)
        forward = jnp.einsum("ksd,sod->kso", col_pieces, wide_tiles) * live_mask[None, :, None]
        backward = jnp.einsum("kso,sod->ksd", row_pieces, wide_tiles) * live_mask[None, :, None]
        forward_sum = forward_sum.at[:, global_rows, :].add(forward)
        backward_sum = backward_sum.at[:, global_cols, :].add(backward)
        return (forward_sum, backward_sum), None

    empty_sum = jnp.zeros((field_rows, DOCS // TILE, TILE), jnp.float32)
    summed, unused = lax.scan(one_device, (empty_sum, empty_sum), (dev_tiles, local_rows, local_cols, live_counts, device_ids))
    forward_sum, backward_sum = summed
    return (0.5 * (forward_sum + backward_sum)).reshape(field_rows, DOCS)


def reference(scores, tile_values, tile_rows, tile_cols, tile_count):
    degree = tile_products(jnp.ones((1, DOCS), jnp.float32), tile_values, tile_rows, tile_cols, tile_count)

    def operate(direction):
        graph_part = tile_products(direction, tile_values, tile_rows, tile_cols, tile_count)
        return direction + coupling * (degree * direction - graph_part)

    solution = jnp.zeros_like(scores)
    residual = scores
    direction = scores
    norm_now = jnp.sum(residual * residual, axis=1)
    for step_index in range(ITERS):
        image_field = operate(direction)
        step_size = norm_now / jnp.sum(direction * image_field, axis=1)
        solution = solution + step_size[:, None] * direction
        residual = residual - step_size[:, None] * image_field
        norm_next = jnp.sum(residual * residual, axis=1)
        direction = residual + (norm_next / norm_now)[:, None] * direction
        norm_now = norm_next
    return solution, residual
```

```python
import functools

import jax
import jax.numpy as jnp
import numpy as np
from jax import lax
from jax.experimental import pallas as pl
from jax.experimental.pallas import tpu as pltpu
from jax.sharding import PartitionSpec as P

PER_ROW = 5
ITERS = 3
MESH_AXES = ("row", "col")

coupling = 0.2

NT = (((1,), (1,)), ((), ()))


def products_kernel(
    task_count, unroll, row_slots, row_loads, row_place, col_slots, col_loads, col_place,
    row_field, col_field, tiles, forward, backward, inner,
):
    row_tiles = row_place.shape[0]
    col_tiles = col_place.shape[0]
    per_row = row_slots.shape[0] // row_tiles
    per_col = col_slots.shape[0] // col_tiles
    ratio = row_tiles // col_tiles
    rows_held = row_field.shape[1]
    forward[...] = jnp.zeros_like(forward)
    inner[...] = jnp.zeros_like(inner)

    def one_row(i):
        base = i * per_row
        field = jnp.concatenate([col_field[row_loads[base + j]] for j in range(per_row)], axis=1)
        block = jnp.concatenate([tiles[row_slots[base + j]] for j in range(per_row)], axis=1)
        total = lax.dot_general(field, block, NT, preferred_element_type=jnp.float32)
        place = row_place[i]
        forward[place] = total
        own = row_field[place][:task_count].astype(jnp.float32)
        part = -own * total[:task_count]
        if rows_held > task_count:
            part += 0.5 * (own * own) * total[task_count : task_count + 1]
        return part

    def one_col(i):
        base = i * per_col
        field = jnp.concatenate([row_field[col_loads[base + j]] for j in range(per_col)], axis=1)
        block = jnp.concatenate([tiles[col_slots[base + j]] for j in range(per_col)], axis=0)
        total = jnp.dot(field, block, preferred_element_type=jnp.float32)
        place = col_place[i]
        backward[place] = total
        if rows_held > task_count:
            own = col_field[place][:task_count].astype(jnp.float32)
            return 0.5 * (own * own) * total[task_count : task_count + 1]
        return None

    def step(g, carry):
        parts = []
        for u in range(unroll):
            i = g * unroll + u
            parts.append(one_col(i))
            for k in range(ratio):
                parts.append(one_row(i * ratio + k))
        inner[...] += sum(p for p in parts if p is not None)
        return carry

    lax.fori_loop(0, col_tiles // unroll, step, 0)


def products(lists, row_field, col_field, tiles, task_count, row_pieces, col_tiles):
    rows_held = row_field.shape[1]
    tile_size = row_field.shape[2]
    unroll = next(u for u in (8, 6, 4, 3, 2, 1) if col_tiles % u == 0)
    in_smem = pl.BlockSpec(memory_space=pltpu.SMEM)
    in_vmem = pl.BlockSpec(memory_space=pltpu.VMEM)
    slots = tiles.shape[0]
    return pl.pallas_call(
        functools.partial(products_kernel, task_count, unroll),
        out_shape=(
            jax.ShapeDtypeStruct((row_pieces, rows_held, tile_size), jnp.float32),
            jax.ShapeDtypeStruct((col_tiles, rows_held, tile_size), jnp.float32),
            jax.ShapeDtypeStruct((task_count, tile_size), jnp.float32),
        ),
        in_specs=[in_smem] * 6 + [in_vmem] * 3,
        out_specs=(in_vmem,) * 3,
        compiler_params=pltpu.CompilerParams(vmem_limit_bytes=44 * 2**20),
        cost_estimate=pl.CostEstimate(
            flops=4 * slots * rows_held * tile_size * tile_size,
            bytes_accessed=2 * slots * tile_size * tile_size,
            transcendentals=0,
        ),
    )(*lists, row_field, col_field, tiles)


def sorted_lists(ids, loads, per_id):
    slots = ids.shape[0]
    order = jnp.arange(slots, dtype=jnp.int32)
    before = (ids[:, None] == ids[None, :]) & (order[None, :] < order[:, None])
    place = ids * per_id + jnp.sum(before, axis=1, dtype=jnp.int32)
    chosen = place[None, :] == order[:, None]
    pick = lambda values: jnp.sum(jnp.where(chosen, values[None, :], 0), axis=1, dtype=jnp.int32)
    return pick(order), pick(loads)


def exact_parts(value, count):
    parts = []
    for _ in range(count):
        high = lax.reduce_precision(value, 8, 7)
        parts.append(high.astype(jnp.bfloat16))
        value = value - high
    return parts


class Plan:
    def __init__(self, rows, cols):
        self.rows, self.cols = rows, cols
        chip_rows = rows // 2
        others = [("row", m) for m in range(1, chip_rows)]
        self.row_steps = len(others)
        partners = [("col", k) for k in range(1, cols)]
        self.steps = (len(others) + len(partners) + 1) // 2
        first = others + partners[: self.steps - len(others)]
        second = partners[self.steps - len(others) :]
        second += [None] * (self.steps - len(second))
        self.gather_steps = list(zip(first, second, strict=True))
        self.sum_steps = [
            (None if a is None or a[0] == "row" else a, b) for a, b in self.gather_steps
        ]
        place = np.zeros((2, cols), np.int32)
        for j, pair in enumerate(self.gather_steps):
            for core, partner in enumerate(pair):
                if partner is not None and partner[0] == "col":
                    place[core, partner[1]] = 1 + j
                    place[1 - core, partner[1]] = 1 + self.steps + j
        self.place = place

    def pairs(self, by_core):
        found = []
        for r in range(self.rows):
            partner = by_core[r % 2]
            if partner is None:
                continue
            axis, k = partner
            for c in range(self.cols):
                to = (r ^ (2 * k), c) if axis == "row" else (r, c ^ k)
                found.append((r * self.cols + c, to[0] * self.cols + to[1]))
        return found

    def send(self, value, by_core):
        return lax.ppermute(value, MESH_AXES, self.pairs(by_core))

    def swap(self, value):
        return lax.ppermute(value, "row", [(r, r ^ 1) for r in range(self.rows)])


def per_device(plan, scores, tile_values, tile_rows, tile_cols, tile_count):
    tiles = tile_values[0, 0]
    row_ids = tile_rows[0, 0]
    col_ids = tile_cols[0, 0]
    live = tile_count[0, 0]
    slots, tile_size = tiles.shape[0], tiles.shape[1]
    task_count, piece_len = scores.shape
    own_tiles = piece_len // tile_size
    row_tiles, col_tiles = own_tiles * plan.cols, own_tiles * plan.rows
    steps = plan.steps
    row_pieces = own_tiles * (1 + 2 * steps)
    row_index, col_index = lax.axis_index("row"), lax.axis_index("col")
    core = row_index % 2
    low = jnp.bfloat16

    place_of = jnp.where(core == 0, jnp.asarray(plan.place[0]), jnp.asarray(plan.place[1]))

    def row_place(ids):
        piece = (ids // own_tiles) ^ col_index
        chosen = piece[:, None] == jnp.arange(plan.cols, dtype=jnp.int32)[None, :]
        piece = jnp.sum(jnp.where(chosen, place_of[None, :], 0), axis=1, dtype=jnp.int32)
        return piece * own_tiles + ids % own_tiles

    def col_place(ids):
        return ((ids // own_tiles) ^ row_index) * own_tiles + ids % own_tiles

    is_live = jnp.arange(slots, dtype=jnp.int32) < live
    row_loads_of = jnp.where(is_live, row_place(row_ids), row_pieces)
    col_loads_of = jnp.where(is_live, col_place(col_ids), col_tiles)
    lists = (
        *sorted_lists(row_ids, col_loads_of, slots // row_tiles),
        row_place(jnp.arange(row_tiles, dtype=jnp.int32)),
        *sorted_lists(col_ids, row_loads_of, slots // col_tiles),
        col_place(jnp.arange(col_tiles, dtype=jnp.int32)),
    )

    def gather(own):
        sibling = plan.swap(own)
        pair = jnp.concatenate([own, sibling])
        got = [plan.send(pair, by_core) for by_core in plan.gather_steps]
        mine = [g[:own_tiles] for g in got]
        other = [g[own_tiles:] for g in got]
        swapped = plan.swap(jnp.concatenate(other + mine[: plan.row_steps]))
        swapped = jnp.split(swapped, steps + plan.row_steps)
        empty = jnp.zeros((1,) + own.shape[1:], own.dtype)
        col_pieces = [own, sibling]
        for m in range(plan.row_steps):
            col_pieces.append(jnp.where(core == 0, mine[m], swapped[m]))
            col_pieces.append(jnp.where(core == 0, other[m], swapped[steps + m]))
        row_field = jnp.concatenate([own] + mine + swapped[:steps] + [empty])
        col_field = jnp.concatenate(col_pieces + [empty])
        return row_field, col_field

    def with_ones(field):
        field = jnp.pad(field[:-1], ((0, 0), (0, 16), (0, 0)), constant_values=1)
        return jnp.pad(field, ((0, 1), (0, 0), (0, 0)))

    def split_dots(dots, rows_held):
        parts = jnp.stack(exact_parts(dots, 3), axis=1).reshape(-1, task_count).T
        parts = jnp.pad(parts, ((0, rows_held - task_count), (0, tile_size - parts.shape[1])))
        return parts[None]

    def join_dots(tile, count):
        parts = tile[0, :task_count, : 3 * count].astype(jnp.float32)
        return jnp.sum(parts.reshape(task_count, count, 3), axis=2).T

    def totals(forward, backward, dots):
        rows_held = forward.shape[1]
        count = dots.shape[0]
        low_part = own_tiles * steps
        extra = rows_held > task_count

        def to_low(value):
            if not extra:
                return value.astype(low)
            rounded = lax.reduce_precision(value, 8, 7)
            at = lax.broadcasted_iota(jnp.int32, value.shape, 1)
            return jnp.where(at == task_count + 1, value - rounded, rounded).astype(low)

        forward_own = forward[:own_tiles]
        forward_low = to_low(forward[own_tiles:])
        backward = backward.reshape(plan.rows // 2, 2, own_tiles, rows_held, tile_size)
        out = [forward_low[low_part:], to_low(backward[:, 1].reshape(-1, rows_held, tile_size))]
        got = plan.swap(jnp.concatenate(out + [split_dots(dots, rows_held)]))
        forward_sibling = got[:low_part]
        backward_sibling = got[low_part:-1].reshape(backward[:, 0].shape)
        dots = dots + join_dots(got[-1:], count)
        dots_tile = split_dots(dots, rows_held)

        mine, other, dots_mine = 0, 0, 0
        for j, by_core in enumerate(plan.sum_steps):
            piece = slice(j * own_tiles, (j + 1) * own_tiles)
            message = jnp.concatenate([forward_low[piece], forward_sibling[piece], dots_tile])
            back = plan.send(message, by_core).astype(jnp.float32)
            mine += back[:own_tiles]
            other += back[own_tiles:-1]
            dots_mine += join_dots(back[-1:], count)
        dots_wide = jnp.pad(
            dots_mine.T, ((0, rows_held - task_count), (0, tile_size - count))
        )[None]
        got = plan.swap(jnp.concatenate([other, dots_wide]))
        dots = dots + dots_mine + got[-1, :task_count, :count].T

        def clean(value):
            if not extra:
                return value
            at = lax.broadcasted_iota(jnp.int32, value.shape, 1)
            return jnp.where(at == task_count + 1, 0.0, value)

        own = clean(forward_own) + mine + got[:-1]
        backward_mine = [
            clean(backward[m, 0]) + backward_sibling[m].astype(jnp.float32)
            for m in range(plan.rows // 2)
        ]
        own += backward_mine[0]
        dots_tile = split_dots(dots, rows_held)
        for m in range(1, plan.rows // 2):
            wide = backward_mine[m]
            if extra:
                joined = wide[:, task_count] + wide[:, task_count + 1]
                at = lax.broadcasted_iota(jnp.int32, wide.shape, 1)
                wide = jnp.where(at == task_count, joined[:, None], wide)
                wide = jnp.where(at == task_count + 1, joined[:, None], wide)
            message = jnp.concatenate([to_low(wide), dots_tile])
            back = plan.send(message, (("row", m),) * 2).astype(jnp.float32)
            own += back[:-1]
            dots = dots + join_dots(back[-1:], count)
        return 0.5 * own, dots

    def inner(a, b):
        return jnp.sum(a * b, axis=(0, 2))

    residual = scores.reshape(task_count, own_tiles, tile_size).transpose(1, 0, 2)
    solution = direction = image = None
    norm_before = curve_before = scale = None
    for step_index in range(ITERS):
        own_low = residual.astype(low)
        first = step_index == 0
        row_field, col_field = gather(own_low)
        if first:
            row_field, col_field = with_ones(row_field), with_ones(col_field)
        forward, backward, inner_part = products(
            lists, row_field, col_field, tiles, task_count, row_pieces, col_tiles
        )
        norm = inner(residual, residual)
        weighted = norm if first else inner(scale * residual, residual)
        along = jnp.zeros_like(norm) if first else inner(residual, image)
        curve_part = weighted + coupling * jnp.sum(inner_part, axis=1)
        summed, dots = totals(forward, backward, jnp.stack([norm, curve_part, along]))
        if first:
            degree = summed[:, task_count : task_count + 1] + summed[:, task_count + 1 : task_count + 2]
            scale = 1.0 + coupling * degree
        norm, curve, along = dots
        fresh = scale * residual - coupling * summed[:, :task_count]
        if first:
            direction, image = residual, fresh
        else:
            ratio = norm / norm_before
            curve = curve + 2.0 * ratio * along + ratio * ratio * curve_before
            direction = residual + ratio[:, None] * direction
            image = fresh + ratio[:, None] * image
        norm_before, curve_before = norm, curve
        step_size = (norm / curve)[:, None]
        solution = step_size * direction if first else solution + step_size * direction
        residual = residual - step_size * image

    def to_field(value):
        return value.transpose(1, 0, 2).reshape(task_count, piece_len)

    return to_field(solution), to_field(residual)


def solution(mesh):
    plan = Plan(mesh.shape["row"], mesh.shape["col"])
    return jax.shard_map(
        functools.partial(per_device, plan),
        mesh=mesh,
        in_specs=(
            P(None, ("row", "col")),
            P("row", "col", None, None, None),
            P("row", "col", None),
            P("row", "col", None),
            P("row", "col"),
        ),
        out_specs=(P(None, ("row", "col")), P(None, ("row", "col"))),
        check_vma=False,
    )
```

```python
import functools

import jax
import jax.numpy as jnp
import numpy as np
from jax import lax
from jax.experimental import pallas as pl
from jax.experimental.pallas import tpu as pltpu
from jax.sharding import PartitionSpec as P

PER_ROW = 5
ITERS = 3
MESH_AXES = ("row", "col")

coupling = 0.2

def start_copies(source, held, semaphores, to_held=True):
    parts = semaphores.shape[0]
    part = source.shape[0] // parts
    copies = []
    for i in range(parts):
        ends = (source.at[pl.ds(i * part, part)], held.at[pl.ds(i * part, part)])
        copies.append(pltpu.make_async_copy(*(ends if to_held else ends[::-1]), semaphores.at[i]))
    if to_held:
        for copy in copies:
            copy.start()
    return copies


def parts_of(count, wanted):
    return next(n for n in range(wanted, 0, -1) if count % n == 0)


def in_steps(count, unroll, one):
    unroll = parts_of(count, unroll)

    def step(g, carry):
        for u in range(unroll):
            one(g * unroll + u)
        return carry

    lax.fori_loop(0, count // unroll, step, 0)


def gathered(field, loads, base, per):
    return jnp.concatenate([field[loads[base + j]] for j in range(per)], axis=1)


def col_kernel(slots, loads, place, field, source, out, tiles, semaphores):
    copies = start_copies(source, tiles, semaphores)
    count = place.shape[0]
    per = slots.shape[0] // count
    for copy in copies:
        copy.wait()

    def one(i):
        base = i * per
        block = jnp.concatenate([tiles[slots[base + j]] for j in range(per)], axis=0)
        held = gathered(field, loads, base, per)
        out[place[i]] = jnp.dot(held, block, preferred_element_type=jnp.float32)

    in_steps(count, 8, one)


def first_row_kernel(
    slots, loads, place, field, source, out, row_blocks, tiles, blocks, semaphores, back_semaphores
):
    copies = start_copies(source, tiles, semaphores)
    back = start_copies(row_blocks, blocks, back_semaphores, to_held=False)
    count = place.shape[0]
    per = slots.shape[0] // count
    tile_size = tiles.shape[1]
    out[...] = jnp.zeros_like(out)
    for copy in copies:
        copy.wait()

    def one(i):
        base = i * per
        for j in range(per):
            blocks[i, pl.ds(j * tile_size, tile_size)] = tiles[slots[base + j]].T
        held = gathered(field, loads, base, per)
        out[place[i]] = jnp.dot(held, blocks[i], preferred_element_type=jnp.float32)

    part = count // len(back)
    for g, copy in enumerate(back):
        in_steps(part, 8, lambda i, g=g: one(g * part + i))
        copy.start()
    for copy in back:
        copy.wait()


def next_row_kernel(loads, place, field, source, out, blocks, semaphores):
    copies = start_copies(source, blocks, semaphores)
    count = place.shape[0]
    per = loads.shape[0] // count
    out[...] = jnp.zeros_like(out)

    def one(i):
        held = gathered(field, loads, i * per, per)
        total = jnp.dot(held, blocks[i], preferred_element_type=jnp.float32)
        out[place[i]] = total.astype(out.dtype)

    part = count // len(copies)
    for g, copy in enumerate(copies):
        copy.wait()
        in_steps(part, 8, lambda i, g=g: one(g * part + i))


IN_SMEM = pl.BlockSpec(memory_space=pltpu.SMEM)
IN_VMEM = pl.BlockSpec(memory_space=pltpu.VMEM)
IN_HBM = pl.BlockSpec(memory_space=pltpu.HBM)
PARAMS = pltpu.CompilerParams(vmem_limit_bytes=48 * 2**20)


def cost(field, tiles):
    return pl.CostEstimate(
        flops=16 * tiles.size * field.shape[1], bytes_accessed=2 * tiles.size, transcendentals=0
    )


def product(lists, field, tiles, out_tiles):
    parts = parts_of(tiles.shape[0], 8)
    return pl.pallas_call(
        col_kernel,
        out_shape=jax.ShapeDtypeStruct((out_tiles,) + field.shape[1:], jnp.float32),
        in_specs=[IN_SMEM] * 3 + [IN_VMEM, IN_HBM],
        out_specs=IN_VMEM,
        scratch_shapes=[pltpu.VMEM(tiles.shape, tiles.dtype), pltpu.SemaphoreType.DMA((parts,))],
        compiler_params=PARAMS,
        cost_estimate=cost(field, tiles),
    )(*lists, field, tiles)


def first_product(lists, field, tiles, out_tiles):
    count = lists[2].shape[0]
    slots, tile_size = tiles.shape[:2]
    blocks = (count, slots // count * tile_size, tile_size)
    return pl.pallas_call(
        first_row_kernel,
        out_shape=(
            jax.ShapeDtypeStruct((out_tiles,) + field.shape[1:], jnp.float32),
            jax.ShapeDtypeStruct(blocks, tiles.dtype),
        ),
        in_specs=[IN_SMEM] * 3 + [IN_VMEM, IN_HBM],
        out_specs=(IN_VMEM, IN_HBM),
        scratch_shapes=[
            pltpu.VMEM(tiles.shape, tiles.dtype),
            pltpu.VMEM(blocks, tiles.dtype),
            pltpu.SemaphoreType.DMA((parts_of(slots, 8),)),
            pltpu.SemaphoreType.DMA((parts_of(count, 6),)),
        ],
        compiler_params=PARAMS,
        cost_estimate=cost(field, tiles),
    )(*lists, field, tiles)


def next_product(lists, field, blocks, out_tiles):
    return pl.pallas_call(
        next_row_kernel,
        out_shape=jax.ShapeDtypeStruct((out_tiles,) + field.shape[1:], field.dtype),
        in_specs=[IN_SMEM] * 2 + [IN_VMEM, IN_HBM],
        out_specs=IN_VMEM,
        scratch_shapes=[
            pltpu.VMEM(blocks.shape, blocks.dtype),
            pltpu.SemaphoreType.DMA((parts_of(blocks.shape[0], 6),)),
        ],
        compiler_params=PARAMS,
        cost_estimate=cost(field, blocks),
    )(*lists[1:], field, blocks)


def sorted_lists(ids, loads, per_id):
    slots = ids.shape[0]
    order = jnp.arange(slots, dtype=jnp.int32)
    before = (ids[:, None] == ids[None, :]) & (order[None, :] < order[:, None])
    place = ids * per_id + jnp.sum(before, axis=1, dtype=jnp.int32)
    chosen = place[None, :] == order[:, None]
    pick = lambda values: jnp.sum(jnp.where(chosen, values[None, :], 0), axis=1, dtype=jnp.int32)
    return pick(order), pick(loads)


def split(value, rows_held):
    parts = []
    for _ in range(3):
        high = lax.reduce_precision(value, 8, 7)
        parts.append(high)
        value = value - high
    parts = jnp.stack(parts).astype(jnp.bfloat16)
    return jnp.pad(parts, ((0, 0), (0, rows_held - parts.shape[1]), (0, 0)))


def join(parts, rows):
    return jnp.sum(parts[:, :rows].astype(jnp.float32), axis=0)


class Plan:
    def __init__(self, rows, cols):
        self.rows, self.cols = rows, cols
        self.row_steps = [("row", m) for m in range(1, rows // 2)]
        first = self.row_steps + [("col", k) for k in range(2, cols, 2)]
        second = [("col", k) for k in range(1, cols, 2)]
        while len(first) > len(second) + 1:
            second.append(first.pop())
        first += [None] * (len(second) - len(first))
        second += [None] * (len(first) - len(second))
        self.count = len(first)
        self.steps = list(zip(first, second, strict=True))
        self.sum_steps = [(None if a in self.row_steps else a, b) for a, b in self.steps]
        place = np.zeros((2, cols), np.int32)
        for j, pair in enumerate(self.steps):
            for core, partner in enumerate(pair):
                if partner is not None and partner[0] == "col":
                    place[core, partner[1]] = 1 + j
                    place[1 - core, partner[1]] = 1 + self.count + j
        self.place = place

    def pairs(self, by_core):
        found = []
        for r in range(self.rows):
            partner = by_core[r % 2]
            if partner is None:
                continue
            axis, k = partner
            for c in range(self.cols):
                to = (r ^ (2 * k), c) if axis == "row" else (r, c ^ k)
                found.append((r * self.cols + c, to[0] * self.cols + to[1]))
        return found

    def send(self, value, by_core):
        return lax.ppermute(value, MESH_AXES, self.pairs(by_core))

    def swap(self, value):
        return lax.ppermute(value, "row", [(r, r ^ 1) for r in range(self.rows)])


def per_device(plan, scores, tile_values, tile_rows, tile_cols, tile_count):
    tiles = tile_values[0, 0]
    row_ids = tile_rows[0, 0]
    col_ids = tile_cols[0, 0]
    live = tile_count[0, 0]
    slots, tile_size = tiles.shape[:2]
    task_count, piece_len = scores.shape
    own_tiles = piece_len // tile_size
    row_tiles, col_tiles = own_tiles * plan.cols, own_tiles * plan.rows
    low_part = own_tiles * plan.count
    row_pieces = own_tiles + 2 * low_part
    row_index, col_index = lax.axis_index("row"), lax.axis_index("col")
    core = row_index % 2
    low = jnp.bfloat16

    place_of = jnp.where(core == 0, jnp.asarray(plan.place[0]), jnp.asarray(plan.place[1]))

    def row_place(ids):
        piece = (ids // own_tiles) ^ col_index
        chosen = piece[:, None] == jnp.arange(plan.cols, dtype=jnp.int32)[None, :]
        piece = jnp.sum(jnp.where(chosen, place_of[None, :], 0), axis=1, dtype=jnp.int32)
        return piece * own_tiles + ids % own_tiles

    def col_place(ids):
        return ((ids // own_tiles) ^ row_index) * own_tiles + ids % own_tiles

    def make_lists(row_ids, col_ids, live):
        is_live = jnp.arange(slots, dtype=jnp.int32) < live
        row_loads_of = jnp.where(is_live, row_place(row_ids), row_pieces)
        col_loads_of = jnp.where(is_live, col_place(col_ids), col_tiles)
        by_row = (
            *sorted_lists(row_ids, col_loads_of, slots // row_tiles),
            row_place(jnp.arange(row_tiles, dtype=jnp.int32)),
        )
        by_col = (
            *sorted_lists(col_ids, row_loads_of, slots // col_tiles),
            col_place(jnp.arange(col_tiles, dtype=jnp.int32)),
        )
        return by_row, by_col

    def empty_tile(field):
        return jnp.zeros((1,) + field.shape[1:], field.dtype)

    def with_ones(field):
        field = jnp.pad(field[:-1], ((0, 0), (0, 16), (0, 0)), constant_values=1)
        return jnp.pad(field, ((0, 1), (0, 0), (0, 0)))

    def to_low(value):
        if value.shape[1] == task_count:
            return value.astype(low)
        rounded = lax.reduce_precision(value, 8, 7)
        at = lax.broadcasted_iota(jnp.int32, value.shape, 1)
        return jnp.where(at == task_count + 1, value - rounded, rounded).astype(low)

    def one_addend(value):
        if value.shape[1] == task_count:
            return value
        at = lax.broadcasted_iota(jnp.int32, value.shape, 1)
        return jnp.where(at == task_count + 1, 0.0, value)

    def two_addends(value):
        return value[:, task_count : task_count + 1] + value[:, task_count + 1 : task_count + 2]

    def inner(a, b):
        return jnp.sum(a.astype(jnp.float32) * b.astype(jnp.float32), axis=(0, 2))[:, None]

    def as_tile(columns):
        at = lax.broadcasted_iota(jnp.int32, (task_count, tile_size), 1)
        return sum(jnp.where(at == i, column, 0.0) for i, column in enumerate(columns))

    near = len(plan.row_steps)
    chip_rows = plan.rows // 2
    residual = scores.reshape(task_count, own_tiles, tile_size).transpose(1, 0, 2)
    solution = direction = image = None
    norm_before = curve_before = scale = None
    for step_index in range(ITERS):
        first = step_index == 0
        at = slice(0, task_count)

        own_low = residual.astype(low)
        pair = jnp.concatenate([own_low, plan.swap(own_low)])
        if first:
            pair, row_ids, col_ids, live = lax.optimization_barrier((pair, row_ids, col_ids, live))
            by_row, by_col = make_lists(row_ids, col_ids, live)
        got = [plan.send(pair, by_core) for by_core in plan.steps]
        shared = [plan.swap(g) for g in got[:near]]
        col_pieces = [pair]
        for g, other in zip(got, shared):
            col_pieces.append(jnp.where(core == 0, g[:own_tiles], other[own_tiles:]))
            col_pieces.append(jnp.where(core == 0, g[own_tiles:], other[:own_tiles]))
        col_field = jnp.concatenate(col_pieces + [empty_tile(pair)])
        if first:
            col_field = with_ones(col_field)
            forward, row_blocks = first_product(by_row, col_field, tiles, row_pieces)
        else:
            forward = next_product(by_row, col_field, row_blocks, row_pieces)

        far, forward = lax.optimization_barrier((got[near:], forward))
        forward = to_low(forward)
        mine = [g[:own_tiles] for g in got[:near] + far]
        swapped = plan.swap(jnp.concatenate([g[own_tiles:] for g in far]))
        row_field = jnp.concatenate(
            [own_low] + mine + [o[own_tiles:] for o in shared] + [swapped, empty_tile(pair)]
        )
        curve_part = -inner(row_field[:-1], forward[:, at])
        if first:
            backward = product(by_col, with_ones(row_field), tiles, col_tiles)
        norm = inner(residual, residual)
        if first:
            square = lambda value: value.astype(jnp.float32) ** 2
            curve_part += 0.5 * inner(
                square(row_field[:-1]), two_addends(forward.astype(jnp.float32))
            )
            curve_part += 0.5 * inner(
                square(col_field[:-1, at]), backward[:, task_count : task_count + 1]
            )
            dots = as_tile([norm, norm + coupling * curve_part])
        else:
            weighted = inner(scale * residual, residual)
            dots = as_tile([norm, weighted + coupling * curve_part, inner(residual, image)])

        rows_held = forward.shape[1]
        swapped = plan.swap(
            jnp.concatenate([forward[own_tiles + low_part :], split(dots, rows_held)])
        )
        if not first:
            swapped, row_field = lax.optimization_barrier((swapped, row_field))
            backward = product(by_col, row_field, tiles, col_tiles)
        dots = dots + join(swapped[low_part:], task_count)
        dots_low = split(dots, rows_held)
        messages = []
        for j, by_core in enumerate(plan.sum_steps):
            piece = slice(j * own_tiles, (j + 1) * own_tiles)
            message = jnp.concatenate([forward[own_tiles:][piece], swapped[piece], dots_low])
            messages.append(plan.send(message, by_core))
        backward = backward.reshape(chip_rows, 2, own_tiles, rows_held, tile_size)
        back = plan.swap(backward[:, 1].reshape(-1, rows_held, tile_size))
        backward = backward[:, 0] + back.reshape(backward[:, 0].shape)
        total = sum(m.astype(jnp.float32) for m in messages)
        dots_mine = jnp.sum(total[2 * own_tiles :], axis=0)
        back = plan.swap(jnp.concatenate([total[own_tiles : 2 * own_tiles], dots_mine[None]]))
        dots = dots + (dots_mine + back[-1])[at]
        total = total[:own_tiles] + back[:-1] + forward[:own_tiles].astype(jnp.float32)

        total = total + one_addend(backward[0])
        dots_low = split(dots, rows_held)
        for m, by_core in enumerate(plan.row_steps, 1):
            message = jnp.concatenate([to_low(backward[m]), dots_low])
            back = plan.send(message, (by_core,) * 2)
            total = total + back[:own_tiles].astype(jnp.float32)
            dots = dots + join(back[own_tiles:], task_count)
        total = 0.5 * total

        norm, curve, along = dots[:, 0:1], dots[:, 1:2], dots[:, 2:3]
        if first:
            scale = 1.0 + coupling * two_addends(total)
        fresh = scale * residual - coupling * total[:, at]
        if first:
            direction, image = residual, fresh
        else:
            ratio = norm / norm_before
            curve = curve + 2.0 * ratio * along + ratio * ratio * curve_before
            direction = residual + ratio * direction
            image = fresh + ratio * image
        norm_before, curve_before = norm, curve
        step_size = norm / curve
        solution = step_size * direction if first else solution + step_size * direction
        residual = residual - step_size * image

    def to_field(value):
        return value.transpose(1, 0, 2).reshape(task_count, piece_len)

    return to_field(solution), to_field(residual)


def solution(mesh):
    plan = Plan(mesh.shape["row"], mesh.shape["col"])
    return jax.shard_map(
        functools.partial(per_device, plan),
        mesh=mesh,
        in_specs=(
            P(None, ("row", "col")),
            P("row", "col", None, None, None),
            P("row", "col", None),
            P("row", "col", None),
            P("row", "col"),
        ),
        out_specs=(P(None, ("row", "col")), P(None, ("row", "col"))),
        check_vma=False,
    )
```

```python
import functools

import jax
import jax.numpy as jnp
import numpy as np
from jax import lax
from jax.experimental import pallas as pl
from jax.experimental.pallas import tpu as pltpu
from jax.sharding import PartitionSpec as P

PER_ROW = 5
ITERS = 3
MESH_AXES = ("row", "col")

coupling = 0.2

def start_copies(source, held, semaphores, to_held=True):
    parts = semaphores.shape[0]
    part = source.shape[0] // parts
    copies = []
    for i in range(parts):
        ends = (source.at[pl.ds(i * part, part)], held.at[pl.ds(i * part, part)])
        copies.append(pltpu.make_async_copy(*(ends if to_held else ends[::-1]), semaphores.at[i]))
    if to_held:
        for copy in copies:
            copy.start()
    return copies


def parts_of(count, wanted):
    return next(n for n in range(wanted, 0, -1) if count % n == 0)


def in_steps(count, unroll, one):
    unroll = parts_of(count, unroll)

    def step(g, carry):
        for u in range(unroll):
            one(g * unroll + u)
        return carry

    lax.fori_loop(0, count // unroll, step, 0)


def gathered(field, loads, base, per):
    return jnp.concatenate([field[loads[base + j]] for j in range(per)], axis=1)


def col_kernel(slots, loads, place, field, source, out, tiles, semaphores):
    copies = start_copies(source, tiles, semaphores)
    count = place.shape[0]
    per = slots.shape[0] // count
    for copy in copies:
        copy.wait()

    def one(i):
        base = i * per
        block = jnp.concatenate([tiles[slots[base + j]] for j in range(per)], axis=0)
        held = gathered(field, loads, base, per)
        out[place[i]] = jnp.dot(held, block, preferred_element_type=jnp.float32)

    in_steps(count, 8, one)


def first_row_kernel(
    slots, loads, place, field, source, out, degree, col_degree, squares, row_blocks, tiles, blocks,
    semaphores, back_semaphores,
):
    copies = start_copies(source, tiles, semaphores)
    back = start_copies(row_blocks, blocks, back_semaphores, to_held=False)
    count = place.shape[0]
    per = slots.shape[0] // count
    tile_size = tiles.shape[1]
    tasks = out.shape[1]
    out[...] = jnp.zeros_like(out)
    degree[...] = jnp.zeros_like(degree)
    squares[...] = jnp.zeros_like(squares)
    col_degree[...] = jnp.zeros_like(col_degree)
    for copy in copies:
        copy.wait()

    def one(i):
        base = i * per
        for j in range(per):
            tile = tiles[slots[base + j]]
            blocks[i, pl.ds(j * tile_size, tile_size)] = tile.T
            addends = tile.astype(jnp.float32).reshape(tile_size // 8, 8, tile_size)
            col_degree[loads[base + j]] += jnp.sum(addends, axis=0)
        held = gathered(field, loads, base, per)
        total = jnp.dot(held, blocks[i], preferred_element_type=jnp.float32)
        out[place[i]] = total[:tasks].astype(out.dtype)
        degree[place[i]] = total[tasks : tasks + 8]
        squares[...] += total[tasks + 16 :]

    part = count // len(back)
    for g, copy in enumerate(back):
        in_steps(part, 8, lambda i, g=g: one(g * part + i))
        copy.start()
    for copy in back:
        copy.wait()


def next_row_kernel(loads, place, field, source, out, blocks, semaphores):
    copies = start_copies(source, blocks, semaphores)
    count = place.shape[0]
    per = loads.shape[0] // count
    out[...] = jnp.zeros_like(out)

    def one(i):
        held = gathered(field, loads, i * per, per)
        total = jnp.dot(held, blocks[i], preferred_element_type=jnp.float32)
        out[place[i]] = total.astype(out.dtype)

    part = count // len(copies)
    for g, copy in enumerate(copies):
        copy.wait()
        in_steps(part, 8, lambda i, g=g: one(g * part + i))


IN_SMEM = pl.BlockSpec(memory_space=pltpu.SMEM)
IN_VMEM = pl.BlockSpec(memory_space=pltpu.VMEM)
IN_HBM = pl.BlockSpec(memory_space=pltpu.HBM)
PARAMS = pltpu.CompilerParams(vmem_limit_bytes=48 * 2**20)


def cost(field, tiles):
    return pl.CostEstimate(
        flops=16 * tiles.size * field.shape[1], bytes_accessed=2 * tiles.size, transcendentals=0
    )


def product(lists, field, tiles, out_tiles):
    parts = parts_of(tiles.shape[0], 8)
    return pl.pallas_call(
        col_kernel,
        out_shape=jax.ShapeDtypeStruct((out_tiles,) + field.shape[1:], jnp.float32),
        in_specs=[IN_SMEM] * 3 + [IN_VMEM, IN_HBM],
        out_specs=IN_VMEM,
        scratch_shapes=[pltpu.VMEM(tiles.shape, tiles.dtype), pltpu.SemaphoreType.DMA((parts,))],
        compiler_params=PARAMS,
        cost_estimate=cost(field, tiles),
    )(*lists, field, tiles)


def first_product(lists, field, tiles, out_tiles, tasks):
    count = lists[2].shape[0]
    slots, tile_size = tiles.shape[:2]
    blocks = (count, slots // count * tile_size, tile_size)
    return pl.pallas_call(
        first_row_kernel,
        out_shape=(
            jax.ShapeDtypeStruct((out_tiles, tasks, tile_size), field.dtype),
            jax.ShapeDtypeStruct((out_tiles, 8, tile_size), jnp.float32),
            jax.ShapeDtypeStruct((field.shape[0], 8, tile_size), jnp.float32),
            jax.ShapeDtypeStruct((tasks, tile_size), jnp.float32),
            jax.ShapeDtypeStruct(blocks, tiles.dtype),
        ),
        in_specs=[IN_SMEM] * 3 + [IN_VMEM, IN_HBM],
        out_specs=(IN_VMEM, IN_VMEM, IN_VMEM, IN_VMEM, IN_HBM),
        scratch_shapes=[
            pltpu.VMEM(tiles.shape, tiles.dtype),
            pltpu.VMEM(blocks, tiles.dtype),
            pltpu.SemaphoreType.DMA((parts_of(slots, 8),)),
            pltpu.SemaphoreType.DMA((parts_of(count, 6),)),
        ],
        compiler_params=PARAMS,
        cost_estimate=cost(field, tiles),
    )(*lists, field, tiles)


def next_product(lists, field, blocks, out_tiles):
    return pl.pallas_call(
        next_row_kernel,
        out_shape=jax.ShapeDtypeStruct((out_tiles,) + field.shape[1:], field.dtype),
        in_specs=[IN_SMEM] * 2 + [IN_VMEM, IN_HBM],
        out_specs=IN_VMEM,
        scratch_shapes=[
            pltpu.VMEM(blocks.shape, blocks.dtype),
            pltpu.SemaphoreType.DMA((parts_of(blocks.shape[0], 6),)),
        ],
        compiler_params=PARAMS,
        cost_estimate=cost(field, blocks),
    )(*lists[1:], field, blocks)


def sorted_lists(ids, loads, per_id):
    slots = ids.shape[0]
    order = jnp.arange(slots, dtype=jnp.int32)
    before = (ids[:, None] == ids[None, :]) & (order[None, :] < order[:, None])
    place = ids * per_id + jnp.sum(before, axis=1, dtype=jnp.int32)
    chosen = place[None, :] == order[:, None]
    pick = lambda values: jnp.sum(jnp.where(chosen, values[None, :], 0), axis=1, dtype=jnp.int32)
    return pick(order), pick(loads)


def addends(value, count):
    parts = []
    for _ in range(count):
        high = lax.reduce_precision(value, 8, 7)
        parts.append(high)
        value = value - high
    return jnp.stack(parts).astype(jnp.bfloat16)


def join(parts):
    return jnp.sum(parts.astype(jnp.float32), axis=0)


def rows_to_tiles(rows, tile_rows):
    count = -(-rows.shape[0] // tile_rows)
    rows = jnp.pad(rows, ((0, count * tile_rows - rows.shape[0]), (0, 0)))
    return rows.reshape(count, tile_rows, rows.shape[1])


def tiles_to_rows(tiles, count):
    return tiles.reshape(-1, tiles.shape[2])[:count]


class Plan:
    def __init__(self, rows, cols):
        self.rows, self.cols = rows, cols
        self.row_steps = [("row", m) for m in range(1, rows // 2)]
        first = self.row_steps + [("col", k) for k in range(cols - 2, 0, -2)]
        second = [("col", 1)] + [("col", k) for k in range(cols - 1, 1, -2)]
        while len(first) > len(second) + 1:
            second.append(first.pop())
        first += [None] * (len(second) - len(first))
        second += [None] * (len(first) - len(second))
        self.count = len(first)
        self.steps = list(zip(first, second, strict=True))
        self.sum_steps = [(None if a in self.row_steps else a, b) for a, b in self.steps]
        place = np.zeros((2, cols), np.int32)
        for j, pair in enumerate(self.steps):
            for core, partner in enumerate(pair):
                if partner is not None and partner[0] == "col":
                    place[core, partner[1]] = 1 + j
                    place[1 - core, partner[1]] = 1 + self.count + j
        self.place = place

    def pairs(self, by_core):
        found = []
        for r in range(self.rows):
            partner = by_core[r % 2]
            if partner is None:
                continue
            axis, k = partner
            for c in range(self.cols):
                to = (r ^ (2 * k), c) if axis == "row" else (r, c ^ k)
                found.append((r * self.cols + c, to[0] * self.cols + to[1]))
        return found

    def send(self, value, by_core):
        return lax.ppermute(value, MESH_AXES, self.pairs(by_core))

    def swap(self, value):
        return lax.ppermute(value, "row", [(r, r ^ 1) for r in range(self.rows)])


def per_device(plan, scores, tile_values, tile_rows, tile_cols, tile_count):
    tiles = tile_values[0, 0]
    row_ids = tile_rows[0, 0]
    col_ids = tile_cols[0, 0]
    live = tile_count[0, 0]
    slots, tile_size = tiles.shape[:2]
    task_count, piece_len = scores.shape
    own_tiles = piece_len // tile_size
    row_tiles, col_tiles = own_tiles * plan.cols, own_tiles * plan.rows
    low_part = own_tiles * plan.count
    row_pieces = own_tiles + 2 * low_part
    row_index, col_index = lax.axis_index("row"), lax.axis_index("col")
    core = row_index % 2
    low = jnp.bfloat16

    place_of = jnp.where(core == 0, jnp.asarray(plan.place[0]), jnp.asarray(plan.place[1]))

    def row_place(ids):
        piece = (ids // own_tiles) ^ col_index
        chosen = piece[:, None] == jnp.arange(plan.cols, dtype=jnp.int32)[None, :]
        piece = jnp.sum(jnp.where(chosen, place_of[None, :], 0), axis=1, dtype=jnp.int32)
        return piece * own_tiles + ids % own_tiles

    def col_place(ids):
        return ((ids // own_tiles) ^ row_index) * own_tiles + ids % own_tiles

    def make_lists(row_ids, col_ids, live):
        is_live = jnp.arange(slots, dtype=jnp.int32) < live
        row_loads_of = jnp.where(is_live, row_place(row_ids), row_pieces)
        col_loads_of = jnp.where(is_live, col_place(col_ids), col_tiles)
        by_row = (
            *sorted_lists(row_ids, col_loads_of, slots // row_tiles),
            row_place(jnp.arange(row_tiles, dtype=jnp.int32)),
        )
        by_col = (
            *sorted_lists(col_ids, row_loads_of, slots // col_tiles),
            col_place(jnp.arange(col_tiles, dtype=jnp.int32)),
        )
        return by_row, by_col

    def empty_tile(field):
        return jnp.zeros((1,) + field.shape[1:], field.dtype)

    def with_rows(field):
        ones = jnp.ones((field.shape[0] - 1, 16, tile_size), field.dtype)
        squares = (field[:-1].astype(jnp.float32) ** 2).astype(field.dtype)
        field = jnp.concatenate([field[:-1], ones, squares], axis=1)
        return jnp.pad(field, ((0, 1), (0, 0), (0, 0)))

    def pack(degree):
        return rows_to_tiles(addends(degree, 2).reshape(-1, tile_size), task_count)

    def unpack(tiles, count):
        return join(tiles_to_rows(tiles, 2 * count).reshape(2, count, tile_size))

    def inner(a, b):
        return jnp.sum(a.astype(jnp.float32) * b.astype(jnp.float32), axis=(0, 2))[:, None]

    def as_tile(columns):
        at = lax.broadcasted_iota(jnp.int32, (task_count, tile_size), 1)
        return sum(jnp.where(at == i, column, 0.0) for i, column in enumerate(columns))

    near = len(plan.row_steps)
    chip_rows = plan.rows // 2
    residual = scores.reshape(task_count, own_tiles, tile_size).transpose(1, 0, 2)
    solution = direction = image = None
    norm_before = curve_before = scale = None
    for step_index in range(ITERS):
        first = step_index == 0

        own_low = residual.astype(low)
        pair = jnp.concatenate([own_low, plan.swap(own_low)])
        if first:
            pair, row_ids, col_ids, live = lax.optimization_barrier((pair, row_ids, col_ids, live))
            by_row, by_col = make_lists(row_ids, col_ids, live)
        got = [plan.send(pair, by_core) for by_core in plan.steps]
        shared = [plan.swap(g) for g in got[:near]]
        col_pieces = [pair]
        for g, other in zip(got, shared):
            col_pieces.append(jnp.where(core == 0, g[:own_tiles], other[own_tiles:]))
            col_pieces.append(jnp.where(core == 0, g[own_tiles:], other[:own_tiles]))
        col_field = jnp.concatenate(col_pieces + [empty_tile(pair)])
        if first:
            forward, row_degree, col_degree, squares, row_blocks = first_product(
                by_row, with_rows(col_field), tiles, row_pieces, task_count
            )
        else:
            forward = next_product(by_row, col_field, row_blocks, row_pieces)

        far, forward = lax.optimization_barrier((got[near:], forward))
        mine = [g[:own_tiles] for g in got[:near] + far]
        swapped = plan.swap(jnp.concatenate([g[own_tiles:] for g in far]))
        row_field = jnp.concatenate(
            [own_low] + mine + [o[own_tiles:] for o in shared] + [swapped, empty_tile(pair)]
        )
        curve_part = -inner(row_field[:-1], forward)
        norm = inner(residual, residual)
        if first:
            row_degree = row_degree[:, 0]
            weights = 0.5 * coupling * row_degree[:, None]
            curve_part = coupling * curve_part
            curve_part += inner(row_field[:-1].astype(jnp.float32) ** 2, weights)
            curve_part += 0.5 * coupling * jnp.sum(squares, axis=1, keepdims=True)
            dots = as_tile([norm, norm + curve_part])
        else:
            weighted = inner(scale * residual, residual)
            dots = as_tile([norm, weighted + coupling * curve_part, inner(residual, image)])

        parts = [forward[own_tiles + low_part :], addends(dots, 3)]
        if first:
            col_degree = jnp.sum(col_degree[:-1], axis=1)
            col_degree = col_degree.reshape(chip_rows, 2, own_tiles, tile_size)
            sent = [row_degree[own_tiles + low_part :], col_degree[:, 1].reshape(-1, tile_size)]
            parts.append(pack(jnp.concatenate(sent)))
        swapped = plan.swap(jnp.concatenate(parts))
        swapped, row_field = lax.optimization_barrier((swapped, row_field))
        if first:
            back = unpack(swapped[low_part + 3 :], low_part + chip_rows * own_tiles)
            other_degree = back[:low_part]
            col_degree = col_degree[:, 0] + back[low_part:].reshape(col_degree[:, 0].shape)
        backward = product(by_col, row_field, tiles, col_tiles)
        dots = dots + join(swapped[low_part : low_part + 3])
        dots_low = addends(dots, 3)
        messages = []
        for j, by_core in enumerate(plan.sum_steps):
            piece = slice(j * own_tiles, (j + 1) * own_tiles)
            message = [forward[own_tiles:][piece], swapped[:low_part][piece], dots_low]
            if first:
                degrees = [row_degree[own_tiles:][piece], other_degree[piece]]
                message.append(pack(jnp.concatenate(degrees)))
            messages.append(plan.send(jnp.concatenate(message), by_core))
        backward = backward.reshape(chip_rows, 2, own_tiles, task_count, tile_size)
        back = plan.swap(backward[:, 1].reshape(-1, task_count, tile_size))
        backward = backward[:, 0] + back.reshape(backward[:, 0].shape)
        total = sum(m.astype(jnp.float32) for m in messages)
        dots_mine = jnp.sum(total[2 * own_tiles : 2 * own_tiles + 3], axis=0)
        message = [total[own_tiles : 2 * own_tiles], dots_mine[None]]
        if first:
            degree = unpack(total[2 * own_tiles + 3 :], 2 * own_tiles)
            message.append(rows_to_tiles(degree[own_tiles:], task_count))
        back = plan.swap(jnp.concatenate(message))
        dots = dots + (dots_mine + back[own_tiles])
        total = total[:own_tiles] + back[:own_tiles] + forward[:own_tiles].astype(jnp.float32)
        if first:
            degree = degree[:own_tiles] + tiles_to_rows(back[own_tiles + 1 :], own_tiles)
            degree += row_degree[:own_tiles] + col_degree[0]

        total = total + backward[0]
        dots_low = addends(dots, 3)
        for m, by_core in enumerate(plan.row_steps, 1):
            message = [backward[m].astype(low), dots_low]
            if first:
                message.append(pack(col_degree[m]))
            back = plan.send(jnp.concatenate(message), (by_core,) * 2)
            total = total + back[:own_tiles].astype(jnp.float32)
            dots = dots + join(back[own_tiles : own_tiles + 3])
            if first:
                degree += unpack(back[own_tiles + 3 :], own_tiles)
        total = 0.5 * total

        norm, curve, along = dots[:, 0:1], dots[:, 1:2], dots[:, 2:3]
        if first:
            scale = 1.0 + 0.5 * coupling * degree[:, None]
        fresh = scale * residual - coupling * total
        if first:
            direction, image = residual, fresh
        else:
            ratio = norm / norm_before
            curve = curve + 2.0 * ratio * along + ratio * ratio * curve_before
            direction = residual + ratio * direction
            image = fresh + ratio * image
        norm_before, curve_before = norm, curve
        step_size = norm / curve
        solution = step_size * direction if first else solution + step_size * direction
        residual = residual - step_size * image

    def to_field(value):
        return value.transpose(1, 0, 2).reshape(task_count, piece_len)

    return to_field(solution), to_field(residual)


def solution(mesh):
    plan = Plan(mesh.shape["row"], mesh.shape["col"])
    return jax.shard_map(
        functools.partial(per_device, plan),
        mesh=mesh,
        in_specs=(
            P(None, ("row", "col")),
            P("row", "col", None, None, None),
            P("row", "col", None),
            P("row", "col", None),
            P("row", "col"),
        ),
        out_specs=(P(None, ("row", "col")), P(None, ("row", "col"))),
        check_vma=False,
    )
```

```python
import functools

import jax
import jax.numpy as jnp
import numpy as np
from jax import lax
from jax.experimental import pallas as pl
from jax.experimental.pallas import tpu as pltpu
from jax.sharding import PartitionSpec as P

PER_ROW = 5
ITERS = 3
MESH_AXES = ("row", "col")

coupling = 0.2

def start_copies(source, held, semaphores, to_held=True):
    parts = semaphores.shape[0]
    part = source.shape[0] // parts
    copies = []
    for i in range(parts):
        ends = (source.at[pl.ds(i * part, part)], held.at[pl.ds(i * part, part)])
        copies.append(pltpu.make_async_copy(*(ends if to_held else ends[::-1]), semaphores.at[i]))
    if to_held:
        for copy in copies:
            copy.start()
    return copies


def parts_of(count, wanted):
    return next(n for n in range(wanted, 0, -1) if count % n == 0)


def fields_kernel(*refs):
    half = len(refs) // 2
    for held, out in zip(refs[:half], refs[half:], strict=True):
        count, rows, tile_size = held.shape
        for i in range(count):
            out[:, pl.ds(i * tile_size, tile_size)] = held[i]


def to_fields(*held):
    count, rows, tile_size = held[0].shape
    return pl.pallas_call(
        fields_kernel,
        out_shape=[jax.ShapeDtypeStruct((rows, count * tile_size), h.dtype) for h in held],
        in_specs=[IN_VMEM] * len(held),
        out_specs=[IN_VMEM] * len(held),
        compiler_params=pltpu.CompilerParams(vmem_limit_bytes=4 * 2**20),
    )(*held)


def in_steps(count, unroll, one):
    unroll = parts_of(count, unroll)

    def step(g, carry):
        for u in range(unroll):
            one(g * unroll + u)
        return carry

    lax.fori_loop(0, count // unroll, step, 0)


def gathered(field, loads, base, per):
    return jnp.concatenate([field[loads[0, base + j]] for j in range(per)], axis=1)


def first_col_kernel(
    per, slots, loads, place, field, source, out, col_blocks, tiles, blocks, semaphores,
    back_semaphores,
):
    copies = start_copies(source, tiles, semaphores)
    back = start_copies(col_blocks, blocks, back_semaphores, to_held=False)
    count = place.shape[0]
    tile_size = tiles.shape[1]
    for copy in copies:
        copy.wait()

    def one(i):
        base = i * per
        for j in range(per):
            blocks[i, pl.ds(j * tile_size, tile_size)] = tiles[slots[0, base + j]]
        held = gathered(field, loads, base, per)
        out[place[i]] = jnp.dot(held, blocks[i], preferred_element_type=jnp.float32)

    part = count // len(back)
    for g, copy in enumerate(back):
        in_steps(part, 4, lambda i, g=g: one(g * part + i))
        copy.start()
    for copy in back:
        copy.wait()


def first_row_kernel(
    per, col_of, slots, loads, place, field, source, out, degree, col_degree, squares, row_blocks, tiles, blocks,
    semaphores, back_semaphores,
):
    copies = start_copies(source, tiles, semaphores)
    back = start_copies(row_blocks, blocks, back_semaphores, to_held=False)
    count = place.shape[0]
    tile_size = tiles.shape[1]
    tasks = out.shape[1]
    out[...] = jnp.zeros_like(out)
    degree[...] = jnp.zeros_like(degree)
    squares[...] = jnp.zeros_like(squares)
    col_degree[...] = jnp.zeros_like(col_degree)

    def add_columns(s):
        addends = tiles[s].astype(jnp.float32).reshape(tile_size // 8, 8, tile_size)
        col_degree[col_of[0, s]] += jnp.sum(addends, axis=0)

    part = tiles.shape[0] // len(copies)
    for g, copy in enumerate(copies):
        copy.wait()
        in_steps(part, 10, lambda s, g=g: add_columns(g * part + s))

    def one(i):
        base = i * per
        for j in range(per):
            blocks[i, pl.ds(j * tile_size, tile_size)] = tiles[slots[0, base + j]].T
        held = gathered(field, loads, base, per)
        total = jnp.dot(held, blocks[i], preferred_element_type=jnp.float32)
        out[place[i]] = total[:tasks].astype(out.dtype)
        degree[place[i]] = total[tasks : tasks + 8]
        squares[...] += total[tasks + 16 :]

    part = count // len(back)
    for g, copy in enumerate(back):
        in_steps(part, 8, lambda i, g=g: one(g * part + i))
        copy.start()
    for copy in back:
        copy.wait()


def next_kernel(per, loads, place, field, source, out, blocks, semaphores):
    copies = start_copies(source, blocks, semaphores)
    count = place.shape[0]
    if out.shape[0] > count:
        out[...] = jnp.zeros_like(out)

    def one(i):
        held = gathered(field, loads, i * per, per)
        total = jnp.dot(held, blocks[i], preferred_element_type=jnp.float32)
        out[place[i]] = total.astype(out.dtype)

    part = count // len(copies)
    for g, copy in enumerate(copies):
        copy.wait()
        in_steps(part, 8, lambda i, g=g: one(g * part + i))


IN_SMEM = pl.BlockSpec(memory_space=pltpu.SMEM)
IN_VMEM = pl.BlockSpec(memory_space=pltpu.VMEM)
IN_HBM = pl.BlockSpec(memory_space=pltpu.HBM)
PARAMS = pltpu.CompilerParams(vmem_limit_bytes=48 * 2**20)


def cost(field, tiles):
    return pl.CostEstimate(
        flops=16 * tiles.size * field.shape[1], bytes_accessed=2 * tiles.size, transcendentals=0
    )


def first_col_product(lists, field, tiles, out_tiles):
    count = lists[2].shape[0]
    slots, tile_size = tiles.shape[:2]
    blocks = (count, slots // count * tile_size, tile_size)
    return pl.pallas_call(
        functools.partial(first_col_kernel, slots // count),
        out_shape=(
            jax.ShapeDtypeStruct((out_tiles,) + field.shape[1:], jnp.float32),
            jax.ShapeDtypeStruct(blocks, tiles.dtype),
        ),
        in_specs=[IN_SMEM] * 3 + [IN_VMEM, IN_HBM],
        out_specs=(IN_VMEM, IN_HBM),
        scratch_shapes=[
            pltpu.VMEM(tiles.shape, tiles.dtype),
            pltpu.VMEM(blocks, tiles.dtype),
            pltpu.SemaphoreType.DMA((parts_of(slots, 8),)),
            pltpu.SemaphoreType.DMA((parts_of(count, 6),)),
        ],
        compiler_params=PARAMS,
        cost_estimate=cost(field, tiles),
    )(*lists, field, tiles)


def first_row_product(col_of, lists, field, tiles, out_tiles, tasks):
    count = lists[2].shape[0]
    slots, tile_size = tiles.shape[:2]
    blocks = (count, slots // count * tile_size, tile_size)
    return pl.pallas_call(
        functools.partial(first_row_kernel, slots // count),
        out_shape=(
            jax.ShapeDtypeStruct((out_tiles, tasks, tile_size), field.dtype),
            jax.ShapeDtypeStruct((out_tiles, 8, tile_size), jnp.float32),
            jax.ShapeDtypeStruct((field.shape[0], 8, tile_size), jnp.float32),
            jax.ShapeDtypeStruct((tasks, tile_size), jnp.float32),
            jax.ShapeDtypeStruct(blocks, tiles.dtype),
        ),
        in_specs=[IN_SMEM] * 4 + [IN_VMEM, IN_HBM],
        out_specs=(IN_VMEM, IN_VMEM, IN_VMEM, IN_VMEM, IN_HBM),
        scratch_shapes=[
            pltpu.VMEM(tiles.shape, tiles.dtype),
            pltpu.VMEM(blocks, tiles.dtype),
            pltpu.SemaphoreType.DMA((parts_of(slots, 8),)),
            pltpu.SemaphoreType.DMA((parts_of(count, 6),)),
        ],
        compiler_params=PARAMS,
        cost_estimate=cost(field, tiles),
    )(col_of, *lists, field, tiles)


def next_product(lists, field, blocks, out_tiles, dtype):
    return pl.pallas_call(
        functools.partial(next_kernel, blocks.shape[1] // blocks.shape[2]),
        out_shape=jax.ShapeDtypeStruct((out_tiles,) + field.shape[1:], dtype),
        in_specs=[IN_SMEM] * 2 + [IN_VMEM, IN_HBM],
        out_specs=IN_VMEM,
        scratch_shapes=[
            pltpu.VMEM(blocks.shape, blocks.dtype),
            pltpu.SemaphoreType.DMA((parts_of(blocks.shape[0], 6),)),
        ],
        compiler_params=PARAMS,
        cost_estimate=cost(field, blocks),
    )(*lists[1:], field, blocks)


def lists_kernel(own_tiles, row_per, col_per, empty, here, row_ids, col_ids, *rest):
    by_row, by_row_loads, by_col, by_col_loads, col_of, ids = rest
    slots = row_ids.shape[1]
    size = ids.shape[1]
    lane = lax.broadcasted_iota(jnp.int32, (1, slots), 1)

    def parts(ids):
        piece = ((ids.astype(jnp.float32) + 0.5) * (1.0 / own_tiles)).astype(jnp.int32)
        return piece, ids - piece * own_tiles

    rows, cols = row_ids[...], col_ids[...]
    piece, inside = parts(rows)
    distance = piece ^ here[0]
    place = sum(
        jnp.where(distance == k, here[3 + k], 0) for k in range(here.shape[0] - 3)
    )
    row_loads = jnp.where(lane < here[2], place * own_tiles + inside, empty[0])
    piece, inside = parts(cols)
    col_loads = jnp.where(lane < here[2], (piece ^ here[1]) * own_tiles + inside, empty[1])
    ids[...] = jnp.full(ids.shape, size, jnp.int32)
    for k, values in enumerate((rows, cols, col_loads, row_loads)):
        ids[k : k + 1, :slots] = values
    across = ids[...]
    col_of[...] = across[2:3]
    down = across.T
    first = lax.broadcasted_iota(jnp.int32, (size, size), 0)
    second = lax.broadcasted_iota(jnp.int32, (size, size), 1)
    for k, per, order, loads in (
        (0, row_per, by_row, by_row_loads),
        (1, col_per, by_col, by_col_loads),
    ):
        key = down[:, k : k + 1]
        before = (key == across[k : k + 1]) & (second < first)
        rank = jnp.sum(before.astype(jnp.float32), axis=1, keepdims=True).astype(jnp.int32)
        chosen = key * per + rank == second
        order[...] = jnp.sum(jnp.where(chosen, first, 0), axis=0, keepdims=True)
        loads[...] = jnp.sum(jnp.where(chosen, down[:, 2 + k : 3 + k], 0), axis=0, keepdims=True)


def sorted_lists(own_tiles, row_per, col_per, empty, here, row_ids, col_ids):
    size = -(-row_ids.shape[1] // 128) * 128
    return pl.pallas_call(
        functools.partial(lists_kernel, own_tiles, row_per, col_per, empty),
        out_shape=[jax.ShapeDtypeStruct((1, size), jnp.int32)] * 5,
        in_specs=[IN_SMEM, IN_VMEM, IN_VMEM],
        out_specs=[IN_VMEM] * 5,
        scratch_shapes=[pltpu.VMEM((8, size), jnp.int32)],
        compiler_params=pltpu.CompilerParams(vmem_limit_bytes=4 * 2**20),
    )(here, row_ids, col_ids)


def addends(value, count):
    parts = []
    for _ in range(count):
        high = lax.reduce_precision(value, 8, 7)
        parts.append(high)
        value = value - high
    return jnp.stack(parts).astype(jnp.bfloat16)


def join(parts):
    return jnp.sum(parts.astype(jnp.float32), axis=0)


def rows_to_tiles(rows, tile_rows):
    count = -(-rows.shape[0] // tile_rows)
    rows = jnp.pad(rows, ((0, count * tile_rows - rows.shape[0]), (0, 0)))
    return rows.reshape(count, tile_rows, rows.shape[1])


def tiles_to_rows(tiles, count):
    return tiles.reshape(-1, tiles.shape[2])[:count]


class Plan:
    def __init__(self, rows, cols):
        self.rows, self.cols = rows, cols
        self.row_steps = [("row", m) for m in range(1, rows // 2)]
        first = self.row_steps + [("col", k) for k in range(cols - 2, 0, -2)]
        second = [("col", 1)] + [("col", k) for k in range(cols - 1, 1, -2)]
        while len(first) > len(second) + 1:
            second.append(first.pop())
        first += [None] * (len(second) - len(first))
        second += [None] * (len(first) - len(second))
        self.count = len(first)
        self.steps = list(zip(first, second, strict=True))
        self.sum_steps = [(None if a in self.row_steps else a, b) for a, b in self.steps]
        place = np.zeros((2, cols), np.int32)
        for j, pair in enumerate(self.steps):
            for core, partner in enumerate(pair):
                if partner is not None and partner[0] == "col":
                    place[core, partner[1]] = 1 + j
                    place[1 - core, partner[1]] = 1 + self.count + j
        self.place = place

    def pairs(self, by_core):
        found = []
        for r in range(self.rows):
            partner = by_core[r % 2]
            if partner is None:
                continue
            axis, k = partner
            for c in range(self.cols):
                to = (r ^ (2 * k), c) if axis == "row" else (r, c ^ k)
                found.append((r * self.cols + c, to[0] * self.cols + to[1]))
        return found

    def send(self, value, by_core):
        return lax.ppermute(value, MESH_AXES, self.pairs(by_core))

    def swap(self, value):
        return lax.ppermute(value, "row", [(r, r ^ 1) for r in range(self.rows)])


def per_device(plan, scores, tile_values, tile_rows, tile_cols, tile_count):
    tiles = tile_values[0, 0]
    row_ids = tile_rows[0]
    col_ids = tile_cols[0]
    live = tile_count[0, 0]
    slots, tile_size = tiles.shape[:2]
    task_count, piece_len = scores.shape
    own_tiles = piece_len // tile_size
    row_tiles, col_tiles = own_tiles * plan.cols, own_tiles * plan.rows
    low_part = own_tiles * plan.count
    row_pieces = own_tiles + 2 * low_part
    row_index, col_index = lax.axis_index("row"), lax.axis_index("col")
    core = row_index % 2
    low = jnp.bfloat16

    place_of = jnp.where(core == 0, jnp.asarray(plan.place[0]), jnp.asarray(plan.place[1]))

    def row_place(ids):
        piece = (ids // own_tiles) ^ col_index
        chosen = piece[:, None] == jnp.arange(plan.cols, dtype=jnp.int32)[None, :]
        piece = jnp.sum(jnp.where(chosen, place_of[None, :], 0), axis=1, dtype=jnp.int32)
        return piece * own_tiles + ids % own_tiles

    def col_place(ids):
        return ((ids // own_tiles) ^ row_index) * own_tiles + ids % own_tiles

    def make_lists(row_ids, col_ids, live):
        here = jnp.concatenate([jnp.stack([col_index, row_index, live]), place_of])
        by_row, by_row_loads, by_col, by_col_loads, col_of = sorted_lists(
            own_tiles, slots // row_tiles, slots // col_tiles, (row_pieces, col_tiles), here,
            row_ids, col_ids,
        )
        by_row = [by_row, by_row_loads, row_place(jnp.arange(row_tiles, dtype=jnp.int32))]
        by_col = [by_col, by_col_loads, col_place(jnp.arange(col_tiles, dtype=jnp.int32))]
        return col_of, by_row, by_col

    def empty_tile(field):
        return jnp.zeros((1,) + field.shape[1:], field.dtype)

    def with_rows(field):
        ones = jnp.ones((field.shape[0] - 1, 16, tile_size), field.dtype)
        squares = (field[:-1].astype(jnp.float32) ** 2).astype(field.dtype)
        field = jnp.concatenate([field[:-1], ones, squares], axis=1)
        return jnp.pad(field, ((0, 1), (0, 0), (0, 0)))

    def pack(degree):
        return rows_to_tiles(addends(degree, 2).reshape(-1, tile_size), task_count)

    def unpack(tiles, count):
        return join(tiles_to_rows(tiles, 2 * count).reshape(2, count, tile_size))

    def inner(a, b):
        return jnp.sum(a.astype(jnp.float32) * b.astype(jnp.float32), axis=(0, 2))[:, None]

    def as_tile(columns):
        at = lax.broadcasted_iota(jnp.int32, (task_count, tile_size), 1)
        return sum(jnp.where(at == i, column, 0.0) for i, column in enumerate(columns))

    near = len(plan.row_steps)
    chip_rows = plan.rows // 2
    chip = 2 * own_tiles
    own = slice(0, own_tiles)
    residual = scores.reshape(task_count, own_tiles, tile_size).transpose(1, 0, 2)
    residual = jnp.concatenate([residual, plan.swap(residual)])
    solution = direction = image = None
    norm_before = curve_before = scale = None
    for step_index in range(ITERS):
        first = step_index == 0

        pair = residual.astype(low)
        if first:
            pair, row_ids, col_ids, live = lax.optimization_barrier((pair, row_ids, col_ids, live))
            col_of, by_row, by_col = make_lists(row_ids, col_ids, live)
        got = [plan.send(pair, by_core) for by_core in plan.steps]
        if first:
            nearby, by_row = lax.optimization_barrier((got[:near], by_row))
            got = nearby + got[near:]
        shared = [plan.swap(g) for g in got[:near]]
        col_pieces = [pair]
        for g, other in zip(got, shared):
            col_pieces.append(jnp.where(core == 0, g[:own_tiles], other[own_tiles:]))
            col_pieces.append(jnp.where(core == 0, g[own_tiles:], other[:own_tiles]))
        col_field = jnp.concatenate(col_pieces + [empty_tile(pair)])
        if first:
            forward, row_degree, col_degree, squares, row_blocks = first_row_product(
                col_of, by_row, with_rows(col_field), tiles, row_pieces, task_count
            )
        else:
            forward = next_product(by_row, col_field, row_blocks, row_pieces, low)

        far, forward = lax.optimization_barrier((got[near:], forward))
        mine = [g[:own_tiles] for g in got[:near] + far]
        swapped = plan.swap(jnp.concatenate([g[own_tiles:] for g in far]))
        row_field = jnp.concatenate(
            [pair[own]] + mine + [o[own_tiles:] for o in shared] + [swapped, empty_tile(pair)]
        )
        curve_part = -inner(row_field[:-1], forward)
        norm = inner(residual[own], residual[own])
        if first:
            row_degree = row_degree[:, 0]
            weights = 0.5 * coupling * row_degree[:, None]
            curve_part = coupling * curve_part
            curve_part += inner(row_field[:-1].astype(jnp.float32) ** 2, weights)
            curve_part += 0.5 * coupling * jnp.sum(squares, axis=1, keepdims=True)
            dots = as_tile([norm, norm + curve_part])
        else:
            weighted = inner(scale[own] * residual[own], residual[own])
            along = inner(residual[own], image[own])
            dots = as_tile([norm, weighted + coupling * curve_part, along])

        parts = [forward[own_tiles + low_part :], addends(dots, 2)]
        if first:
            col_degree = jnp.sum(col_degree[:-1], axis=1).reshape(chip_rows, chip, tile_size)
            parts.append(pack(row_degree[own_tiles + low_part :]))
        swapped = plan.swap(jnp.concatenate(parts))
        swapped, row_field = lax.optimization_barrier((swapped, row_field))
        if first:
            other_degree = unpack(swapped[low_part + 2 :], low_part)
        if first:
            backward, col_blocks = first_col_product(by_col, row_field, tiles, col_tiles)
        else:
            backward = next_product(by_col, row_field, col_blocks, col_tiles, jnp.float32)
        dots = dots + join(swapped[low_part : low_part + 2])
        dots_low = addends(dots, 2)
        mine_products = forward[own]
        messages = []
        order = list(range(plan.count))
        for j in order[1:] + order[:1]:
            by_core = plan.sum_steps[j]
            piece = slice(j * own_tiles, (j + 1) * own_tiles)
            message = [forward[own_tiles:][piece], swapped[:low_part][piece], dots_low]
            if first:
                degrees = [row_degree[own_tiles:][piece], other_degree[piece]]
                message.append(pack(jnp.concatenate(degrees)))
            messages.append(plan.send(jnp.concatenate(message), by_core))

        backward = backward.reshape(chip_rows, chip, task_count, tile_size)
        returned = []
        for m, by_core in enumerate(plan.row_steps, 1):
            returned.append(plan.send(backward[m].astype(low), (by_core,) * 2))
        total = sum(m.astype(jnp.float32) for m in messages)
        dots = jnp.where(core == 0, dots, 0.0) + jnp.sum(total[chip : chip + 2], axis=0)
        dots_mine = dots
        degree_back = col_degree[0] if first else None
        for m, by_core in enumerate(plan.row_steps, 1):
            message = jnp.concatenate([dots_mine, col_degree[m]]) if first else dots_mine
            back = plan.send(message, (by_core,) * 2)
            dots = dots + back[:task_count]
            if first:
                degree_back = degree_back + back[task_count:]
        if first:
            degree = unpack(total[chip + 2 :], chip) + degree_back
            degree += jnp.pad(row_degree[own], ((0, own_tiles), (0, 0)))
        total = total[:chip] + backward[0]
        total += jnp.pad(mine_products.astype(jnp.float32), ((0, own_tiles), (0, 0), (0, 0)))
        total += sum(back.astype(jnp.float32) for back in returned)

        message = [total, dots[None]]
        if first:
            message.append(rows_to_tiles(degree, task_count))
        back = plan.swap(jnp.concatenate(message))
        total = 0.5 * (total + jnp.concatenate([back[own_tiles:chip], back[own]]))
        dots = dots + back[chip]
        if first:
            back = tiles_to_rows(back[chip + 1 :], chip)
            degree = degree + jnp.concatenate([back[own_tiles:], back[own]])

        norm, curve, along = dots[:, 0:1], dots[:, 1:2], dots[:, 2:3]
        if first:
            scale = 1.0 + 0.5 * coupling * degree[:, None]
        fresh = scale * residual - coupling * total
        if first:
            direction, image = residual, fresh
        else:
            ratio = norm / norm_before
            curve = curve + 2.0 * ratio * along + ratio * ratio * curve_before
            direction = residual + ratio * direction
            image = fresh + ratio * image
        norm_before, curve_before = norm, curve
        step_size = norm / curve
        solution = step_size * direction if first else solution + step_size * direction
        residual = residual - step_size * image

    return tuple(to_fields(solution[own], residual[own]))


def solution(mesh):
    plan = Plan(mesh.shape["row"], mesh.shape["col"])
    return jax.shard_map(
        functools.partial(per_device, plan),
        mesh=mesh,
        in_specs=(
            P(None, ("row", "col")),
            P("row", "col", None, None, None),
            P("row", "col", None),
            P("row", "col", None),
            P("row", "col"),
        ),
        out_specs=(P(None, ("row", "col")), P(None, ("row", "col"))),
        check_vma=False,
    )
```

```python
import functools

import jax
import jax.numpy as jnp
import numpy as np
from jax import lax
from jax.experimental import pallas as pl
from jax.experimental.pallas import tpu as pltpu
from jax.sharding import PartitionSpec as P

PER_ROW = 5
ITERS = 3
DOTS = 3
MESH_AXES = ("row", "col")

coupling = 0.2

def start_copies(source, held, semaphores, to_held=True):
    parts = semaphores.shape[0]
    part = source.shape[0] // parts
    copies = []
    for i in range(parts):
        ends = (source.at[pl.ds(i * part, part)], held.at[pl.ds(i * part, part)])
        copies.append(pltpu.make_async_copy(*(ends if to_held else ends[::-1]), semaphores.at[i]))
    if to_held:
        for copy in copies:
            copy.start()
    return copies


def parts_of(count, wanted):
    return next(n for n in range(wanted, 0, -1) if count % n == 0)


def fields_kernel(*refs):
    half = len(refs) // 2
    for held, out in zip(refs[:half], refs[half:], strict=True):
        count, rows, tile_size = held.shape
        for i in range(count):
            out[:, pl.ds(i * tile_size, tile_size)] = held[i]


def to_fields(*held):
    count, rows, tile_size = held[0].shape
    return pl.pallas_call(
        fields_kernel,
        out_shape=[jax.ShapeDtypeStruct((rows, count * tile_size), h.dtype) for h in held],
        in_specs=[IN_VMEM] * len(held),
        out_specs=[IN_VMEM] * len(held),
        compiler_params=pltpu.CompilerParams(vmem_limit_bytes=4 * 2**20),
    )(*held)


def in_steps(count, unroll, one):
    unroll = parts_of(count, unroll)

    def step(g, carry):
        for u in range(unroll):
            one(g * unroll + u)
        return carry

    lax.fori_loop(0, count // unroll, step, 0)


def gathered(field, loads, base, per):
    return jnp.concatenate([field[loads[0, base + j]] for j in range(per)], axis=1)


def first_col_kernel(
    per, slots, loads, place, field, source, out, col_blocks, tiles, blocks, semaphores,
    back_semaphores,
):
    copies = start_copies(source, tiles, semaphores)
    back = start_copies(col_blocks, blocks, back_semaphores, to_held=False)
    count = place.shape[0]
    tile_size = tiles.shape[1]
    for copy in copies:
        copy.wait()

    def one(i):
        base = i * per
        for j in range(per):
            blocks[i, pl.ds(j * tile_size, tile_size)] = tiles[slots[0, base + j]]
        held = gathered(field, loads, base, per)
        out[place[i]] = jnp.dot(held, blocks[i], preferred_element_type=jnp.float32)

    part = count // len(back)
    for g, copy in enumerate(back):
        in_steps(part, 4, lambda i, g=g: one(g * part + i))
        copy.start()
    for copy in back:
        copy.wait()


def first_row_kernel(
    per, col_of, slots, loads, place, field, source, out, degree, col_degree, row_blocks, tiles, blocks,
    semaphores, back_semaphores,
):
    copies = start_copies(source, tiles, semaphores)
    back = start_copies(row_blocks, blocks, back_semaphores, to_held=False)
    count = place.shape[0]
    tile_size = tiles.shape[1]
    tasks = out.shape[1]
    out[...] = jnp.zeros_like(out)
    degree[...] = jnp.zeros_like(degree)
    col_degree[...] = jnp.zeros_like(col_degree)

    def add_columns(s):
        addends = tiles[s].astype(jnp.float32).reshape(tile_size // 8, 8, tile_size)
        col_degree[col_of[0, s]] += jnp.sum(addends, axis=0)

    part = tiles.shape[0] // len(copies)
    for g, copy in enumerate(copies):
        copy.wait()
        in_steps(part, 10, lambda s, g=g: add_columns(g * part + s))

    def one(i):
        base = i * per
        for j in range(per):
            blocks[i, pl.ds(j * tile_size, tile_size)] = tiles[slots[0, base + j]].T
        held = gathered(field, loads, base, per)
        total = jnp.dot(held, blocks[i], preferred_element_type=jnp.float32)
        out[place[i]] = total[:tasks].astype(out.dtype)
        degree[place[i]] = total[tasks : tasks + 8]

    part = count // len(back)
    for g, copy in enumerate(back):
        in_steps(part, 8, lambda i, g=g: one(g * part + i))
        copy.start()
    for copy in back:
        copy.wait()


def next_kernel(per, loads, place, field, source, out, blocks, semaphores):
    copies = start_copies(source, blocks, semaphores)
    count = place.shape[0]
    if out.shape[0] > count:
        out[...] = jnp.zeros_like(out)

    def one(i):
        held = gathered(field, loads, i * per, per)
        total = jnp.dot(held, blocks[i], preferred_element_type=jnp.float32)
        out[place[i]] = total.astype(out.dtype)

    part = count // len(copies)
    for g, copy in enumerate(copies):
        copy.wait()
        in_steps(part, 8, lambda i, g=g: one(g * part + i))


IN_SMEM = pl.BlockSpec(memory_space=pltpu.SMEM)
IN_VMEM = pl.BlockSpec(memory_space=pltpu.VMEM)
IN_HBM = pl.BlockSpec(memory_space=pltpu.HBM)
PARAMS = pltpu.CompilerParams(vmem_limit_bytes=48 * 2**20)


def cost(field, tiles):
    return pl.CostEstimate(
        flops=16 * tiles.size * field.shape[1], bytes_accessed=2 * tiles.size, transcendentals=0
    )


def first_col_product(lists, field, tiles, out_tiles):
    count = lists[2].shape[0]
    slots, tile_size = tiles.shape[:2]
    blocks = (count, slots // count * tile_size, tile_size)
    return pl.pallas_call(
        functools.partial(first_col_kernel, slots // count),
        out_shape=(
            jax.ShapeDtypeStruct((out_tiles,) + field.shape[1:], jnp.float32),
            jax.ShapeDtypeStruct(blocks, tiles.dtype),
        ),
        in_specs=[IN_SMEM] * 3 + [IN_VMEM, IN_HBM],
        out_specs=(IN_VMEM, IN_HBM),
        scratch_shapes=[
            pltpu.VMEM(tiles.shape, tiles.dtype),
            pltpu.VMEM(blocks, tiles.dtype),
            pltpu.SemaphoreType.DMA((parts_of(slots, 8),)),
            pltpu.SemaphoreType.DMA((parts_of(count, 6),)),
        ],
        compiler_params=PARAMS,
        cost_estimate=cost(field, tiles),
    )(*lists, field, tiles)


def first_row_product(col_of, lists, field, tiles, out_tiles, tasks):
    count = lists[2].shape[0]
    slots, tile_size = tiles.shape[:2]
    blocks = (count, slots // count * tile_size, tile_size)
    return pl.pallas_call(
        functools.partial(first_row_kernel, slots // count),
        out_shape=(
            jax.ShapeDtypeStruct((out_tiles, tasks, tile_size), field.dtype),
            jax.ShapeDtypeStruct((out_tiles, 8, tile_size), jnp.float32),
            jax.ShapeDtypeStruct((field.shape[0], 8, tile_size), jnp.float32),
            jax.ShapeDtypeStruct(blocks, tiles.dtype),
        ),
        in_specs=[IN_SMEM] * 4 + [IN_VMEM, IN_HBM],
        out_specs=(IN_VMEM, IN_VMEM, IN_VMEM, IN_HBM),
        scratch_shapes=[
            pltpu.VMEM(tiles.shape, tiles.dtype),
            pltpu.VMEM(blocks, tiles.dtype),
            pltpu.SemaphoreType.DMA((parts_of(slots, 8),)),
            pltpu.SemaphoreType.DMA((parts_of(count, 12),)),
        ],
        compiler_params=PARAMS,
        cost_estimate=cost(field, tiles),
    )(col_of, *lists, field, tiles)


def next_product(lists, field, blocks, out_tiles, dtype):
    return pl.pallas_call(
        functools.partial(next_kernel, blocks.shape[1] // blocks.shape[2]),
        out_shape=jax.ShapeDtypeStruct((out_tiles,) + field.shape[1:], dtype),
        in_specs=[IN_SMEM] * 2 + [IN_VMEM, IN_HBM],
        out_specs=IN_VMEM,
        scratch_shapes=[
            pltpu.VMEM(blocks.shape, blocks.dtype),
            pltpu.SemaphoreType.DMA((parts_of(blocks.shape[0], 6),)),
        ],
        compiler_params=PARAMS,
        cost_estimate=cost(field, blocks),
    )(*lists[1:], field, blocks)


def lists_kernel(own_tiles, row_per, col_per, empty, here, row_source, col_source, *rest):
    by_row, by_row_loads, by_col, by_col_loads, col_of, ids, row_ids, col_ids, semaphores = rest
    copies = [
        pltpu.make_async_copy(row_source, row_ids, semaphores.at[0]),
        pltpu.make_async_copy(col_source, col_ids, semaphores.at[1]),
    ]
    for copy in copies:
        copy.start()
    for copy in copies:
        copy.wait()
    slots = row_ids.shape[1]
    size = ids.shape[1]
    lane = lax.broadcasted_iota(jnp.int32, (1, slots), 1)

    def parts(ids):
        piece = ((ids.astype(jnp.float32) + 0.5) * (1.0 / own_tiles)).astype(jnp.int32)
        return piece, ids - piece * own_tiles

    rows, cols = row_ids[...], col_ids[...]
    piece, inside = parts(rows)
    distance = piece ^ here[0]
    place = sum(
        jnp.where(distance == k, here[3 + k], 0) for k in range(here.shape[0] - 3)
    )
    row_loads = jnp.where(lane < here[2], place * own_tiles + inside, empty[0])
    piece, inside = parts(cols)
    col_loads = jnp.where(lane < here[2], (piece ^ here[1]) * own_tiles + inside, empty[1])
    ids[...] = jnp.full(ids.shape, size, jnp.int32)
    for k, values in enumerate((rows, cols, col_loads, row_loads)):
        ids[k : k + 1, :slots] = values
    across = ids[...]
    col_of[...] = across[2:3]
    down = across.T
    first = lax.broadcasted_iota(jnp.int32, (size, size), 0)
    second = lax.broadcasted_iota(jnp.int32, (size, size), 1)
    for k, per, order, loads in (
        (0, row_per, by_row, by_row_loads),
        (1, col_per, by_col, by_col_loads),
    ):
        key = down[:, k : k + 1]
        before = (key == across[k : k + 1]) & (second < first)
        rank = jnp.sum(before.astype(jnp.float32), axis=1, keepdims=True).astype(jnp.int32)
        chosen = key * per + rank == second
        order[...] = jnp.sum(jnp.where(chosen, first, 0), axis=0, keepdims=True)
        loads[...] = jnp.sum(jnp.where(chosen, down[:, 2 + k : 3 + k], 0), axis=0, keepdims=True)


def sorted_lists(own_tiles, row_per, col_per, empty, here, row_ids, col_ids):
    size = -(-row_ids.shape[1] // 128) * 128
    return pl.pallas_call(
        functools.partial(lists_kernel, own_tiles, row_per, col_per, empty),
        out_shape=[jax.ShapeDtypeStruct((1, size), jnp.int32)] * 5,
        in_specs=[IN_SMEM, IN_HBM, IN_HBM],
        out_specs=[IN_VMEM] * 5,
        scratch_shapes=[
            pltpu.VMEM((8, size), jnp.int32),
            pltpu.VMEM(row_ids.shape, jnp.int32),
            pltpu.VMEM(row_ids.shape, jnp.int32),
            pltpu.SemaphoreType.DMA((2,)),
        ],
        compiler_params=PARAMS,
    )(here, row_ids, col_ids)


def addends(value, count):
    parts = []
    for _ in range(count):
        high = lax.reduce_precision(value, 8, 7)
        parts.append(high)
        value = value - high
    return jnp.stack(parts).astype(jnp.bfloat16)


def join(parts):
    return jnp.sum(parts.astype(jnp.float32), axis=0)


def rows_to_tiles(rows, tile_rows):
    count = -(-rows.shape[0] // tile_rows)
    rows = jnp.pad(rows, ((0, count * tile_rows - rows.shape[0]), (0, 0)))
    return rows.reshape(count, tile_rows, rows.shape[1])


def tiles_to_rows(tiles, count):
    return tiles.reshape(-1, tiles.shape[2])[:count]


class Plan:
    def __init__(self, rows, cols):
        self.rows, self.cols = rows, cols
        self.row_steps = [("row", m) for m in range(1, rows // 2)]
        first = self.row_steps + [("col", k) for k in range(cols - 2, 0, -2)]
        second = [("col", 1)] + [("col", k) for k in range(cols - 1, 1, -2)]
        while len(first) > len(second) + 1:
            second.append(first.pop())
        first += [None] * (len(second) - len(first))
        second += [None] * (len(first) - len(second))
        self.count = len(first)
        self.steps = list(zip(first, second, strict=True))
        self.sum_steps = [(None if a in self.row_steps else a, b) for a, b in self.steps]
        place = np.zeros((2, cols), np.int32)
        for j, pair in enumerate(self.steps):
            for core, partner in enumerate(pair):
                if partner is not None and partner[0] == "col":
                    place[core, partner[1]] = 1 + j
                    place[1 - core, partner[1]] = 1 + self.count + j
        self.place = place

    def pairs(self, by_core):
        found = []
        for r in range(self.rows):
            partner = by_core[r % 2]
            if partner is None:
                continue
            axis, k = partner
            for c in range(self.cols):
                to = (r ^ (2 * k), c) if axis == "row" else (r, c ^ k)
                found.append((r * self.cols + c, to[0] * self.cols + to[1]))
        return found

    def send(self, value, by_core):
        return lax.ppermute(value, MESH_AXES, self.pairs(by_core))

    def swap(self, value):
        return lax.ppermute(value, "row", [(r, r ^ 1) for r in range(self.rows)])


def per_device(plan, scores, tile_values, tile_rows, tile_cols, tile_count):
    tiles = tile_values[0, 0]
    row_ids = tile_rows[0]
    col_ids = tile_cols[0]
    live = tile_count[0, 0]
    slots, tile_size = tiles.shape[:2]
    task_count, piece_len = scores.shape
    own_tiles = piece_len // tile_size
    row_tiles, col_tiles = own_tiles * plan.cols, own_tiles * plan.rows
    low_part = own_tiles * plan.count
    row_pieces = own_tiles + 2 * low_part
    row_index, col_index = lax.axis_index("row"), lax.axis_index("col")
    core = row_index % 2
    low = jnp.bfloat16

    place_of = jnp.where(core == 0, jnp.asarray(plan.place[0]), jnp.asarray(plan.place[1]))

    def row_place(ids):
        piece = (ids // own_tiles) ^ col_index
        chosen = piece[:, None] == jnp.arange(plan.cols, dtype=jnp.int32)[None, :]
        piece = jnp.sum(jnp.where(chosen, place_of[None, :], 0), axis=1, dtype=jnp.int32)
        return piece * own_tiles + ids % own_tiles

    def col_place(ids):
        return ((ids // own_tiles) ^ row_index) * own_tiles + ids % own_tiles

    def make_lists(row_ids, col_ids, live):
        here = jnp.concatenate([jnp.stack([col_index, row_index, live]), place_of])
        by_row, by_row_loads, by_col, by_col_loads, col_of = sorted_lists(
            own_tiles, slots // row_tiles, slots // col_tiles, (row_pieces, col_tiles), here,
            row_ids, col_ids,
        )
        by_row = [by_row, by_row_loads, row_place(jnp.arange(row_tiles, dtype=jnp.int32))]
        by_col = [by_col, by_col_loads, col_place(jnp.arange(col_tiles, dtype=jnp.int32))]
        return col_of, by_row, by_col

    def empty_tile(field):
        return jnp.zeros((1,) + field.shape[1:], field.dtype)

    def with_ones(field):
        field = jnp.pad(field[:-1], ((0, 0), (0, 16), (0, 0)), constant_values=1)
        return jnp.pad(field, ((0, 1), (0, 0), (0, 0)))

    def pack(degree):
        return rows_to_tiles(addends(degree, 2).reshape(-1, tile_size), task_count)

    def unpack(tiles, count):
        return join(tiles_to_rows(tiles, 2 * count).reshape(2, count, tile_size))

    def pack_dots(dots):
        parts = addends(dots, 2)
        return (parts[0] + jnp.pad(parts[1, :, :-DOTS], ((0, 0), (DOTS, 0))))[None]

    def unpack_dots(tile):
        tile = tile.astype(jnp.float32)
        tile = tile + jnp.pad(tile[:, DOTS:], ((0, 0), (0, DOTS)))
        return jnp.where(lax.broadcasted_iota(jnp.int32, tile.shape, 1) < DOTS, tile, 0.0)

    def inner(a, b):
        return jnp.sum(a.astype(jnp.float32) * b.astype(jnp.float32), axis=(0, 2))[:, None]

    def as_tile(columns):
        at = lax.broadcasted_iota(jnp.int32, (task_count, tile_size), 1)
        return sum(jnp.where(at == i, column, 0.0) for i, column in enumerate(columns))

    near = len(plan.row_steps)
    chip_rows = plan.rows // 2
    chip = 2 * own_tiles
    own = slice(0, own_tiles)
    residual = scores.reshape(task_count, own_tiles, tile_size).transpose(1, 0, 2)
    residual = jnp.concatenate([residual, plan.swap(residual)])
    solution = direction = image = None
    norm_before = curve_before = scale = None
    for step_index in range(ITERS):
        first = step_index == 0

        pair = residual.astype(low)
        if first:
            pair, row_ids, col_ids, live = lax.optimization_barrier((pair, row_ids, col_ids, live))
            col_of, by_row, by_col = make_lists(row_ids, col_ids, live)
        got = [plan.send(pair, by_core) for by_core in plan.steps]
        if first:
            nearby, by_row = lax.optimization_barrier((got[:near], by_row))
            got = nearby + got[near:]
        shared = [plan.swap(g) for g in got[:near]]
        col_pieces = [pair]
        for g, other in zip(got, shared):
            col_pieces.append(jnp.where(core == 0, g[:own_tiles], other[own_tiles:]))
            col_pieces.append(jnp.where(core == 0, g[own_tiles:], other[:own_tiles]))
        col_field = jnp.concatenate(col_pieces + [empty_tile(pair)])
        if first:
            forward, row_degree, col_degree, row_blocks = first_row_product(
                col_of, by_row, with_ones(col_field), tiles, row_pieces, task_count
            )
        else:
            forward = next_product(by_row, col_field, row_blocks, row_pieces, low)

        far, forward = lax.optimization_barrier((got[near:], forward))
        mine = [g[:own_tiles] for g in got[:near] + far]
        swapped = plan.swap(jnp.concatenate([g[own_tiles:] for g in far]))
        row_field = jnp.concatenate(
            [pair[own]] + mine + [o[own_tiles:] for o in shared] + [swapped, empty_tile(pair)]
        )
        curve_part = -inner(row_field[:-1], forward)
        norm = inner(residual[own], residual[own])
        if first:
            row_degree = row_degree[:, 0]
            weights = 0.5 * coupling * row_degree[:, None]
            curve_part = coupling * curve_part
            curve_part += inner(row_field[:-1].astype(jnp.float32) ** 2, weights)
            col_degree = jnp.sum(col_degree[:-1], axis=1)
            weights = 0.5 * coupling * col_degree[:, None]
            curve_part += inner(col_field[:-1].astype(jnp.float32) ** 2, weights)
            dots = as_tile([norm, norm + curve_part])
        else:
            weighted = inner(scale[own] * residual[own], residual[own])
            along = inner(residual[own], image[own])
            dots = as_tile([norm, weighted + coupling * curve_part, along])

        parts = [forward[own_tiles + low_part :], pack_dots(dots)]
        if first:
            col_degree = col_degree.reshape(chip_rows, chip, tile_size)
            parts.append(pack(row_degree[own_tiles + low_part :]))
        swapped = plan.swap(jnp.concatenate(parts))
        swapped, row_field = lax.optimization_barrier((swapped, row_field))
        if first:
            other_degree = unpack(swapped[low_part + 1 :], low_part)
        if first:
            backward, col_blocks = first_col_product(by_col, row_field, tiles, col_tiles)
        else:
            backward = next_product(by_col, row_field, col_blocks, col_tiles, jnp.float32)
        dots = dots + unpack_dots(swapped[low_part])
        dots_low = pack_dots(dots)
        mine_products = forward[own]
        messages = []
        order = list(range(plan.count))
        for j in order[1:] + order[:1]:
            by_core = plan.sum_steps[j]
            piece = slice(j * own_tiles, (j + 1) * own_tiles)
            message = [forward[own_tiles:][piece], swapped[:low_part][piece], dots_low]
            if first:
                degrees = [row_degree[own_tiles:][piece], other_degree[piece]]
                message.append(pack(jnp.concatenate(degrees)))
            messages.append(plan.send(jnp.concatenate(message), by_core))

        backward = backward.reshape(chip_rows, chip, task_count, tile_size)
        returned = []
        for m, by_core in enumerate(plan.row_steps, 1):
            returned.append(plan.send(backward[m].astype(low), (by_core,) * 2))
        total = sum(m.astype(jnp.float32) for m in messages)
        dots = jnp.where(core == 0, dots, 0.0) + unpack_dots(total[chip])
        dots_mine = dots
        degree_back = col_degree[0] if first else None
        for m, by_core in enumerate(plan.row_steps, 1):
            message = jnp.concatenate([dots_mine, col_degree[m]]) if first else dots_mine
            back = plan.send(message, (by_core,) * 2)
            dots = dots + back[:task_count]
            if first:
                degree_back = degree_back + back[task_count:]
        if first:
            degree = unpack(total[chip + 1 :], chip) + degree_back
            degree += jnp.pad(row_degree[own], ((0, own_tiles), (0, 0)))
        total = total[:chip] + backward[0]
        total += jnp.pad(mine_products.astype(jnp.float32), ((0, own_tiles), (0, 0), (0, 0)))
        total += sum(back.astype(jnp.float32) for back in returned)

        message = [total, dots[None]]
        if first:
            message.append(rows_to_tiles(degree, task_count))
        back = plan.swap(jnp.concatenate(message))
        total = 0.5 * (total + jnp.concatenate([back[own_tiles:chip], back[own]]))
        dots = dots + back[chip]
        if first:
            back = tiles_to_rows(back[chip + 1 :], chip)
            degree = degree + jnp.concatenate([back[own_tiles:], back[own]])

        norm, curve, along = dots[:, 0:1], dots[:, 1:2], dots[:, 2:3]
        if first:
            scale = 1.0 + 0.5 * coupling * degree[:, None]
        fresh = scale * residual - coupling * total
        if first:
            direction, image = residual, fresh
        else:
            ratio = norm / norm_before
            curve = curve + 2.0 * ratio * along + ratio * ratio * curve_before
            direction = residual + ratio * direction
            image = fresh + ratio * image
        norm_before, curve_before = norm, curve
        step_size = norm / curve
        solution = step_size * direction if first else solution + step_size * direction
        residual = residual - step_size * image

    return tuple(to_fields(solution[own], residual[own]))


def solution(mesh):
    plan = Plan(mesh.shape["row"], mesh.shape["col"])
    return jax.shard_map(
        functools.partial(per_device, plan),
        mesh=mesh,
        in_specs=(
            P(None, ("row", "col")),
            P("row", "col", None, None, None),
            P("row", "col", None),
            P("row", "col", None),
            P("row", "col"),
        ),
        out_specs=(P(None, ("row", "col")), P(None, ("row", "col"))),
        check_vma=False,
    )
```

```python
import functools

import jax
import jax.numpy as jnp
import numpy as np
from jax import lax
from jax.experimental import pallas as pl
from jax.experimental.pallas import tpu as pltpu
from jax.sharding import PartitionSpec as P

PER_ROW = 5
ITERS = 3
DOTS = 3
MESH_AXES = ("row", "col")

coupling = 0.2

def start_copies(source, held, semaphores, to_held=True):
    parts = semaphores.shape[0]
    part = source.shape[0] // parts
    copies = []
    for i in range(parts):
        ends = (source.at[pl.ds(i * part, part)], held.at[pl.ds(i * part, part)])
        copies.append(pltpu.make_async_copy(*(ends if to_held else ends[::-1]), semaphores.at[i]))
    if to_held:
        for copy in copies:
            copy.start()
    return copies


def parts_of(count, wanted):
    return next(n for n in range(wanted, 0, -1) if count % n == 0)


def fields_kernel(*refs):
    half = len(refs) // 2
    for held, out in zip(refs[:half], refs[half:], strict=True):
        count, rows, tile_size = held.shape
        for i in range(count):
            out[:, pl.ds(i * tile_size, tile_size)] = held[i]


def to_fields(*held):
    count, rows, tile_size = held[0].shape
    return pl.pallas_call(
        fields_kernel,
        out_shape=[jax.ShapeDtypeStruct((rows, count * tile_size), h.dtype) for h in held],
        in_specs=[IN_VMEM] * len(held),
        out_specs=[IN_VMEM] * len(held),
        compiler_params=pltpu.CompilerParams(vmem_limit_bytes=4 * 2**20),
    )(*held)


def in_steps(count, unroll, one):
    unroll = parts_of(count, unroll)

    def step(g, carry):
        for u in range(unroll):
            one(g * unroll + u)
        return carry

    lax.fori_loop(0, count // unroll, step, 0)


def gathered(field, loads, base, per):
    return jnp.concatenate([field[loads[0, base + j]] for j in range(per)], axis=1)


def first_col_kernel(
    per, slots, loads, place, field, source, out, col_blocks, tiles, blocks, semaphores,
    back_semaphores,
):
    copies = start_copies(source, tiles, semaphores)
    back = start_copies(col_blocks, blocks, back_semaphores, to_held=False)
    count = place.shape[0]
    tile_size = tiles.shape[1]
    for copy in copies:
        copy.wait()

    def one(i):
        base = i * per
        for j in range(per):
            blocks[i, pl.ds(j * tile_size, tile_size)] = tiles[slots[0, base + j]]
        held = gathered(field, loads, base, per)
        out[place[i]] = jnp.dot(held, blocks[i], preferred_element_type=jnp.float32)

    part = count // len(back)
    for g, copy in enumerate(back):
        in_steps(part, 4, lambda i, g=g: one(g * part + i))
        copy.start()
    for copy in back:
        copy.wait()


def first_row_kernel(
    per, col_of, slots, loads, place, field, source, out, degree, col_degree, row_blocks, tiles, blocks,
    semaphores, back_semaphores,
):
    copies = start_copies(source, tiles, semaphores)
    back = start_copies(row_blocks, blocks, back_semaphores, to_held=False)
    count = place.shape[0]
    tile_size = tiles.shape[1]
    tasks = out.shape[1]
    out[...] = jnp.zeros_like(out)
    degree[...] = jnp.zeros_like(degree)
    col_degree[...] = jnp.zeros_like(col_degree)

    def add_columns(s):
        addends = tiles[s].astype(jnp.float32).reshape(tile_size // 8, 8, tile_size)
        col_degree[col_of[0, s]] += jnp.sum(addends, axis=0)

    part = tiles.shape[0] // len(copies)
    for g, copy in enumerate(copies):
        copy.wait()
        in_steps(part, 10, lambda s, g=g: add_columns(g * part + s))

    def one(i):
        base = i * per
        turned = []
        for j in range(per):
            turned.append(tiles[slots[0, base + j]].T)
        turned = jnp.concatenate(turned, axis=0)
        blocks[i] = turned
        held = gathered(field, loads, base, per)
        total = jnp.dot(held, turned, preferred_element_type=jnp.float32)
        out[place[i]] = total[:tasks].astype(out.dtype)
        degree[place[i]] = total[tasks : tasks + 8]

    part = count // len(back)
    for g, copy in enumerate(back):
        in_steps(part, 8, lambda i, g=g: one(g * part + i))
        copy.start()
    for copy in back:
        copy.wait()


def next_kernel(per, loads, place, field, source, out, blocks, semaphores):
    copies = start_copies(source, blocks, semaphores)
    count = place.shape[0]
    if out.shape[0] > count:
        out[...] = jnp.zeros_like(out)

    def one(i):
        held = gathered(field, loads, i * per, per)
        total = jnp.dot(held, blocks[i], preferred_element_type=jnp.float32)
        out[place[i]] = total.astype(out.dtype)

    part = count // len(copies)
    for g, copy in enumerate(copies):
        copy.wait()
        in_steps(part, 8, lambda i, g=g: one(g * part + i))


IN_SMEM = pl.BlockSpec(memory_space=pltpu.SMEM)
IN_VMEM = pl.BlockSpec(memory_space=pltpu.VMEM)
IN_HBM = pl.BlockSpec(memory_space=pltpu.HBM)
PARAMS = pltpu.CompilerParams(vmem_limit_bytes=48 * 2**20)


def cost(field, tiles):
    return pl.CostEstimate(
        flops=16 * tiles.size * field.shape[1], bytes_accessed=2 * tiles.size, transcendentals=0
    )


def first_col_product(lists, field, tiles, out_tiles):
    count = lists[2].shape[0]
    slots, tile_size = tiles.shape[:2]
    blocks = (count, slots // count * tile_size, tile_size)
    return pl.pallas_call(
        functools.partial(first_col_kernel, slots // count),
        out_shape=(
            jax.ShapeDtypeStruct((out_tiles,) + field.shape[1:], jnp.float32),
            jax.ShapeDtypeStruct(blocks, tiles.dtype),
        ),
        in_specs=[IN_SMEM] * 3 + [IN_VMEM, IN_HBM],
        out_specs=(IN_VMEM, IN_HBM),
        scratch_shapes=[
            pltpu.VMEM(tiles.shape, tiles.dtype),
            pltpu.VMEM(blocks, tiles.dtype),
            pltpu.SemaphoreType.DMA((parts_of(slots, 8),)),
            pltpu.SemaphoreType.DMA((parts_of(count, 6),)),
        ],
        compiler_params=PARAMS,
        cost_estimate=cost(field, tiles),
    )(*lists, field, tiles)


def first_row_product(col_of, lists, field, tiles, out_tiles, tasks):
    count = lists[2].shape[0]
    slots, tile_size = tiles.shape[:2]
    blocks = (count, slots // count * tile_size, tile_size)
    return pl.pallas_call(
        functools.partial(first_row_kernel, slots // count),
        out_shape=(
            jax.ShapeDtypeStruct((out_tiles, tasks, tile_size), field.dtype),
            jax.ShapeDtypeStruct((out_tiles, 8, tile_size), jnp.float32),
            jax.ShapeDtypeStruct((field.shape[0], 8, tile_size), jnp.float32),
            jax.ShapeDtypeStruct(blocks, tiles.dtype),
        ),
        in_specs=[IN_SMEM] * 4 + [IN_VMEM, IN_HBM],
        out_specs=(IN_VMEM, IN_VMEM, IN_VMEM, IN_HBM),
        scratch_shapes=[
            pltpu.VMEM(tiles.shape, tiles.dtype),
            pltpu.VMEM(blocks, tiles.dtype),
            pltpu.SemaphoreType.DMA((parts_of(slots, 8),)),
            pltpu.SemaphoreType.DMA((parts_of(count, 12),)),
        ],
        compiler_params=PARAMS,
        cost_estimate=cost(field, tiles),
    )(col_of, *lists, field, tiles)


def next_product(lists, field, blocks, out_tiles, dtype):
    return pl.pallas_call(
        functools.partial(next_kernel, blocks.shape[1] // blocks.shape[2]),
        out_shape=jax.ShapeDtypeStruct((out_tiles,) + field.shape[1:], dtype),
        in_specs=[IN_SMEM] * 2 + [IN_VMEM, IN_HBM],
        out_specs=IN_VMEM,
        scratch_shapes=[
            pltpu.VMEM(blocks.shape, blocks.dtype),
            pltpu.SemaphoreType.DMA((parts_of(blocks.shape[0], 6),)),
        ],
        compiler_params=PARAMS,
        cost_estimate=cost(field, blocks),
    )(*lists[1:], field, blocks)


def lists_kernel(own_tiles, row_per, col_per, empty, here, row_source, col_source, *rest):
    by_row, by_row_loads, by_col, by_col_loads, col_of, ids, row_ids, col_ids, semaphores = rest
    copies = [
        pltpu.make_async_copy(row_source, row_ids, semaphores.at[0]),
        pltpu.make_async_copy(col_source, col_ids, semaphores.at[1]),
    ]
    for copy in copies:
        copy.start()
    for copy in copies:
        copy.wait()
    slots = row_ids.shape[1]
    size = ids.shape[1]
    lane = lax.broadcasted_iota(jnp.int32, (1, slots), 1)

    def parts(ids):
        piece = ((ids.astype(jnp.float32) + 0.5) * (1.0 / own_tiles)).astype(jnp.int32)
        return piece, ids - piece * own_tiles

    rows, cols = row_ids[...], col_ids[...]
    piece, inside = parts(rows)
    distance = piece ^ here[0]
    place = sum(
        jnp.where(distance == k, here[3 + k], 0) for k in range(here.shape[0] - 3)
    )
    row_loads = jnp.where(lane < here[2], place * own_tiles + inside, empty[0])
    piece, inside = parts(cols)
    col_loads = jnp.where(lane < here[2], (piece ^ here[1]) * own_tiles + inside, empty[1])
    ids[...] = jnp.full(ids.shape, size, jnp.int32)
    for k, values in enumerate((rows, cols, col_loads, row_loads)):
        ids[k : k + 1, :slots] = values
    across = ids[...]
    col_of[...] = across[2:3]
    down = across.T
    first = lax.broadcasted_iota(jnp.int32, (size, size), 0)
    second = lax.broadcasted_iota(jnp.int32, (size, size), 1)
    for k, per, order, loads in (
        (0, row_per, by_row, by_row_loads),
        (1, col_per, by_col, by_col_loads),
    ):
        key = down[:, k : k + 1]
        before = (key == across[k : k + 1]) & (second < first)
        rank = jnp.sum(before.astype(jnp.float32), axis=1, keepdims=True).astype(jnp.int32)
        chosen = key * per + rank == second
        order[...] = jnp.sum(jnp.where(chosen, first, 0), axis=0, keepdims=True)
        loads[...] = jnp.sum(jnp.where(chosen, down[:, 2 + k : 3 + k], 0), axis=0, keepdims=True)


def sorted_lists(own_tiles, row_per, col_per, empty, here, row_ids, col_ids):
    size = -(-row_ids.shape[1] // 128) * 128
    return pl.pallas_call(
        functools.partial(lists_kernel, own_tiles, row_per, col_per, empty),
        out_shape=[jax.ShapeDtypeStruct((1, size), jnp.int32)] * 5,
        in_specs=[IN_SMEM, IN_HBM, IN_HBM],
        out_specs=[IN_VMEM] * 5,
        scratch_shapes=[
            pltpu.VMEM((8, size), jnp.int32),
            pltpu.VMEM(row_ids.shape, jnp.int32),
            pltpu.VMEM(row_ids.shape, jnp.int32),
            pltpu.SemaphoreType.DMA((2,)),
        ],
        compiler_params=PARAMS,
    )(here, row_ids, col_ids)


def addends(value, count):
    parts = []
    for _ in range(count):
        high = lax.reduce_precision(value, 8, 7)
        parts.append(high)
        value = value - high
    return jnp.stack(parts).astype(jnp.bfloat16)


def join(parts):
    return jnp.sum(parts.astype(jnp.float32), axis=0)


def rows_to_tiles(rows, tile_rows):
    count = -(-rows.shape[0] // tile_rows)
    rows = jnp.pad(rows, ((0, count * tile_rows - rows.shape[0]), (0, 0)))
    return rows.reshape(count, tile_rows, rows.shape[1])


def tiles_to_rows(tiles, count):
    return tiles.reshape(-1, tiles.shape[2])[:count]


class Plan:
    def __init__(self, rows, cols):
        self.rows, self.cols = rows, cols
        self.row_steps = [("row", m) for m in range(1, rows // 2)]
        first = self.row_steps + [("col", k) for k in range(cols - 2, 0, -2)]
        second = [("col", 1)] + [("col", k) for k in range(cols - 1, 1, -2)]
        while len(first) > len(second) + 1:
            second.append(first.pop())
        first += [None] * (len(second) - len(first))
        second += [None] * (len(first) - len(second))
        self.count = len(first)
        self.steps = list(zip(first, second, strict=True))
        self.sum_steps = [(None if a in self.row_steps else a, b) for a, b in self.steps]
        place = np.zeros((2, cols), np.int32)
        for j, pair in enumerate(self.steps):
            for core, partner in enumerate(pair):
                if partner is not None and partner[0] == "col":
                    place[core, partner[1]] = 1 + j
                    place[1 - core, partner[1]] = 1 + self.count + j
        self.place = place

    def pairs(self, by_core):
        found = []
        for r in range(self.rows):
            partner = by_core[r % 2]
            if partner is None:
                continue
            axis, k = partner
            for c in range(self.cols):
                to = (r ^ (2 * k), c) if axis == "row" else (r, c ^ k)
                found.append((r * self.cols + c, to[0] * self.cols + to[1]))
        return found

    def send(self, value, by_core):
        return lax.ppermute(value, MESH_AXES, self.pairs(by_core))

    def swap(self, value):
        return lax.ppermute(value, "row", [(r, r ^ 1) for r in range(self.rows)])


def per_device(plan, scores, tile_values, tile_rows, tile_cols, tile_count):
    tiles = tile_values[0, 0]
    row_ids = tile_rows[0]
    col_ids = tile_cols[0]
    live = tile_count[0, 0]
    slots, tile_size = tiles.shape[:2]
    task_count, piece_len = scores.shape
    own_tiles = piece_len // tile_size
    row_tiles, col_tiles = own_tiles * plan.cols, own_tiles * plan.rows
    low_part = own_tiles * plan.count
    row_pieces = own_tiles + 2 * low_part
    row_index, col_index = lax.axis_index("row"), lax.axis_index("col")
    core = row_index % 2
    low = jnp.bfloat16

    place_of = jnp.where(core == 0, jnp.asarray(plan.place[0]), jnp.asarray(plan.place[1]))

    def row_place(ids):
        piece = (ids // own_tiles) ^ col_index
        chosen = piece[:, None] == jnp.arange(plan.cols, dtype=jnp.int32)[None, :]
        piece = jnp.sum(jnp.where(chosen, place_of[None, :], 0), axis=1, dtype=jnp.int32)
        return piece * own_tiles + ids % own_tiles

    def col_place(ids):
        return ((ids // own_tiles) ^ row_index) * own_tiles + ids % own_tiles

    def make_lists(row_ids, col_ids, live):
        here = jnp.concatenate([jnp.stack([col_index, row_index, live]), place_of])
        by_row, by_row_loads, by_col, by_col_loads, col_of = sorted_lists(
            own_tiles, slots // row_tiles, slots // col_tiles, (row_pieces, col_tiles), here,
            row_ids, col_ids,
        )
        by_row = [by_row, by_row_loads, row_place(jnp.arange(row_tiles, dtype=jnp.int32))]
        by_col = [by_col, by_col_loads, col_place(jnp.arange(col_tiles, dtype=jnp.int32))]
        return col_of, by_row, by_col

    def empty_tile(field):
        return jnp.zeros((1,) + field.shape[1:], field.dtype)

    def with_ones(field):
        field = jnp.pad(field[:-1], ((0, 0), (0, 16), (0, 0)), constant_values=1)
        return jnp.pad(field, ((0, 1), (0, 0), (0, 0)))

    def pack(degree):
        return rows_to_tiles(addends(degree, 2).reshape(-1, tile_size), task_count)

    def unpack(tiles, count):
        return join(tiles_to_rows(tiles, 2 * count).reshape(2, count, tile_size))

    def pack_dots(dots):
        parts = addends(dots, 2)
        return (parts[0] + jnp.pad(parts[1, :, :-DOTS], ((0, 0), (DOTS, 0))))[None]

    def unpack_dots(tile):
        tile = tile.astype(jnp.float32)
        tile = tile + jnp.pad(tile[:, DOTS:], ((0, 0), (0, DOTS)))
        return jnp.where(lax.broadcasted_iota(jnp.int32, tile.shape, 1) < DOTS, tile, 0.0)

    def inner(a, b):
        return jnp.sum(a.astype(jnp.float32) * b.astype(jnp.float32), axis=(0, 2))[:, None]

    def as_tile(columns):
        at = lax.broadcasted_iota(jnp.int32, (task_count, tile_size), 1)
        return sum(jnp.where(at == i, column, 0.0) for i, column in enumerate(columns))

    near = len(plan.row_steps)
    chip_rows = plan.rows // 2
    chip = 2 * own_tiles
    own = slice(0, own_tiles)
    residual = scores.reshape(task_count, own_tiles, tile_size).transpose(1, 0, 2)
    residual = jnp.concatenate([residual, plan.swap(residual)])
    solution = direction = image = None
    norm_before = curve_before = scale = None
    for step_index in range(ITERS):
        first = step_index == 0

        pair = residual.astype(low)
        if first:
            pair, row_ids, col_ids, live = lax.optimization_barrier((pair, row_ids, col_ids, live))
            col_of, by_row, by_col = make_lists(row_ids, col_ids, live)
        got = [plan.send(pair, by_core) for by_core in plan.steps]
        if first:
            nearby, by_row = lax.optimization_barrier((got[:near], by_row))
            got = nearby + got[near:]
        shared = [plan.swap(g) for g in got[:near]]
        col_pieces = [pair]
        for g, other in zip(got, shared):
            col_pieces.append(jnp.where(core == 0, g[:own_tiles], other[own_tiles:]))
            col_pieces.append(jnp.where(core == 0, g[own_tiles:], other[:own_tiles]))
        col_field = jnp.concatenate(col_pieces + [empty_tile(pair)])
        if first:
            forward, row_degree, col_degree, row_blocks = first_row_product(
                col_of, by_row, with_ones(col_field), tiles, row_pieces, task_count
            )
        else:
            forward = next_product(by_row, col_field, row_blocks, row_pieces, low)

        far, forward = lax.optimization_barrier((got[near:], forward))
        mine = [g[:own_tiles] for g in got[:near] + far]
        swapped = plan.swap(jnp.concatenate([g[own_tiles:] for g in far]))
        row_field = jnp.concatenate(
            [pair[own]] + mine + [o[own_tiles:] for o in shared] + [swapped, empty_tile(pair)]
        )
        curve_part = -inner(row_field[:-1], forward)
        norm = inner(residual[own], residual[own])
        if first:
            row_degree = row_degree[:, 0]
            weights = 0.5 * coupling * row_degree[:, None]
            curve_part = coupling * curve_part
            curve_part += inner(row_field[:-1].astype(jnp.float32) ** 2, weights)
            col_degree = jnp.sum(col_degree[:-1], axis=1)
            weights = 0.5 * coupling * col_degree[:, None]
            curve_part += inner(col_field[:-1].astype(jnp.float32) ** 2, weights)
            dots = as_tile([norm, norm + curve_part])
        else:
            weighted = inner(scale[own] * residual[own], residual[own])
            along = inner(residual[own], image[own])
            dots = as_tile([norm, weighted + coupling * curve_part, along])

        parts = [forward[own_tiles + low_part :], pack_dots(dots)]
        if first:
            col_degree = col_degree.reshape(chip_rows, chip, tile_size)
            parts.append(pack(row_degree[own_tiles + low_part :]))
        swapped = plan.swap(jnp.concatenate(parts))
        swapped, row_field = lax.optimization_barrier((swapped, row_field))
        if first:
            other_degree = unpack(swapped[low_part + 1 :], low_part)
        if first:
            backward, col_blocks = first_col_product(by_col, row_field, tiles, col_tiles)
        else:
            backward = next_product(by_col, row_field, col_blocks, col_tiles, jnp.float32)
        dots = dots + unpack_dots(swapped[low_part])
        dots_low = pack_dots(dots)
        mine_products = forward[own]
        messages = []
        order = list(range(plan.count))
        for j in order[1:] + order[:1]:
            by_core = plan.sum_steps[j]
            piece = slice(j * own_tiles, (j + 1) * own_tiles)
            message = [forward[own_tiles:][piece], swapped[:low_part][piece], dots_low]
            if first:
                degrees = [row_degree[own_tiles:][piece], other_degree[piece]]
                message.append(pack(jnp.concatenate(degrees)))
            messages.append(plan.send(jnp.concatenate(message), by_core))

        backward = backward.reshape(chip_rows, chip, task_count, tile_size)
        returned = []
        for m, by_core in enumerate(plan.row_steps, 1):
            returned.append(plan.send(backward[m].astype(low), (by_core,) * 2))
        total = sum(m.astype(jnp.float32) for m in messages)
        dots = jnp.where(core == 0, dots, 0.0) + unpack_dots(total[chip])
        dots_mine = dots
        degree_back = col_degree[0] if first else None
        for m, by_core in enumerate(plan.row_steps, 1):
            message = jnp.concatenate([dots_mine, col_degree[m]]) if first else dots_mine
            back = plan.send(message, (by_core,) * 2)
            dots = dots + back[:task_count]
            if first:
                degree_back = degree_back + back[task_count:]
        if first:
            degree = unpack(total[chip + 1 :], chip) + degree_back
            degree += jnp.pad(row_degree[own], ((0, own_tiles), (0, 0)))
        total = total[:chip] + backward[0]
        total += jnp.pad(mine_products.astype(jnp.float32), ((0, own_tiles), (0, 0), (0, 0)))
        total += sum(back.astype(jnp.float32) for back in returned)

        message = [total, dots[None]]
        if first:
            message.append(rows_to_tiles(degree, task_count))
        back = plan.swap(jnp.concatenate(message))
        total = 0.5 * (total + jnp.concatenate([back[own_tiles:chip], back[own]]))
        dots = dots + back[chip]
        if first:
            back = tiles_to_rows(back[chip + 1 :], chip)
            degree = degree + jnp.concatenate([back[own_tiles:], back[own]])

        norm, curve, along = dots[:, 0:1], dots[:, 1:2], dots[:, 2:3]
        if first:
            scale = 1.0 + 0.5 * coupling * degree[:, None]
        fresh = scale * residual - coupling * total
        if first:
            direction, image = residual, fresh
        else:
            ratio = norm / norm_before
            curve = curve + 2.0 * ratio * along + ratio * ratio * curve_before
            direction = residual + ratio * direction
            image = fresh + ratio * image
        norm_before, curve_before = norm, curve
        step_size = norm / curve
        solution = step_size * direction if first else solution + step_size * direction
        residual = residual - step_size * image

    return tuple(to_fields(solution[own], residual[own]))


def solution(mesh):
    plan = Plan(mesh.shape["row"], mesh.shape["col"])
    return jax.shard_map(
        functools.partial(per_device, plan),
        mesh=mesh,
        in_specs=(
            P(None, ("row", "col")),
            P("row", "col", None, None, None),
            P("row", "col", None),
            P("row", "col", None),
            P("row", "col"),
        ),
        out_specs=(P(None, ("row", "col")), P(None, ("row", "col"))),
        check_vma=False,
    )
```

```python
import functools

import jax
import jax.numpy as jnp
import numpy as np
from jax import lax
from jax.experimental import pallas as pl
from jax.experimental.pallas import tpu as pltpu
from jax.sharding import PartitionSpec as P

PER_ROW = 5
ITERS = 3
DOTS = 3
MESH_AXES = ("row", "col")

coupling = 0.2

def start_copies(source, held, semaphores, to_held=True):
    parts = semaphores.shape[0]
    part = source.shape[0] // parts
    copies = []
    for i in range(parts):
        ends = (source.at[pl.ds(i * part, part)], held.at[pl.ds(i * part, part)])
        copies.append(pltpu.make_async_copy(*(ends if to_held else ends[::-1]), semaphores.at[i]))
    if to_held:
        for copy in copies:
            copy.start()
    return copies


def parts_of(count, wanted):
    return next(n for n in range(wanted, 0, -1) if count % n == 0)


def fields_kernel(*refs):
    half = len(refs) // 2
    for held, out in zip(refs[:half], refs[half:], strict=True):
        count, rows, tile_size = held.shape
        for i in range(count):
            out[:, pl.ds(i * tile_size, tile_size)] = held[i]


def to_fields(*held):
    count, rows, tile_size = held[0].shape
    return pl.pallas_call(
        fields_kernel,
        out_shape=[jax.ShapeDtypeStruct((rows, count * tile_size), h.dtype) for h in held],
        in_specs=[IN_VMEM] * len(held),
        out_specs=[IN_VMEM] * len(held),
        compiler_params=pltpu.CompilerParams(vmem_limit_bytes=4 * 2**20),
    )(*held)


def in_steps(count, unroll, one):
    unroll = parts_of(count, unroll)

    def step(g, carry):
        for u in range(unroll):
            one(g * unroll + u)
        return carry

    lax.fori_loop(0, count // unroll, step, 0)


def gathered(field, loads, base, per):
    return jnp.concatenate([field[loads[0, base + j]] for j in range(per)], axis=1)


def first_col_kernel(
    per, slots, loads, place, field, source, out, col_blocks, tiles, blocks, semaphores,
    back_semaphores,
):
    copies = start_copies(source, tiles, semaphores)
    back = start_copies(col_blocks, blocks, back_semaphores, to_held=False)
    count = place.shape[0]
    tile_size = tiles.shape[1]
    for copy in copies:
        copy.wait()

    def one(i):
        base = i * per
        for j in range(per):
            blocks[i, pl.ds(j * tile_size, tile_size)] = tiles[slots[0, base + j]]
        held = gathered(field, loads, base, per)
        out[place[i]] = jnp.dot(held, blocks[i], preferred_element_type=jnp.float32)

    part = count // len(back)
    for g, copy in enumerate(back):
        in_steps(part, 4, lambda i, g=g: one(g * part + i))
        copy.start()
    for copy in back:
        copy.wait()


def first_row_kernel(
    per, col_of, slots, loads, place, field, source, out, degree, col_degree, row_blocks, tiles, blocks,
    semaphores, back_semaphores,
):
    copies = start_copies(source, tiles, semaphores)
    back = start_copies(row_blocks, blocks, back_semaphores, to_held=False)
    count = place.shape[0]
    tile_size = tiles.shape[1]
    tasks = out.shape[1]
    out[...] = jnp.zeros_like(out)
    degree[...] = jnp.zeros_like(degree)
    col_degree[...] = jnp.zeros_like(col_degree)

    def add_columns(s):
        addends = tiles[s].astype(jnp.float32).reshape(tile_size // 8, 8, tile_size)
        col_degree[col_of[0, s]] += jnp.sum(addends, axis=0)

    part = tiles.shape[0] // len(copies)
    for g, copy in enumerate(copies):
        copy.wait()
        in_steps(part, 10, lambda s, g=g: add_columns(g * part + s))

    def one(i):
        base = i * per
        turned = []
        for j in range(per):
            turned.append(tiles[slots[0, base + j]].T)
        turned = jnp.concatenate(turned, axis=0)
        blocks[i] = turned
        held = gathered(field, loads, base, per)
        total = jnp.dot(held, turned, preferred_element_type=jnp.float32)
        out[place[i]] = total[:tasks].astype(out.dtype)
        degree[place[i]] = total[tasks : tasks + 8]

    part = count // len(back)
    for g, copy in enumerate(back):
        in_steps(part, 8, lambda i, g=g: one(g * part + i))
        copy.start()
    for copy in back:
        copy.wait()


def next_kernel(per, loads, place, field, source, out, blocks, semaphores):
    copies = start_copies(source, blocks, semaphores)
    count = place.shape[0]
    if out.shape[0] > count:
        out[...] = jnp.zeros_like(out)

    def one(i):
        held = gathered(field, loads, i * per, per)
        total = jnp.dot(held, blocks[i], preferred_element_type=jnp.float32)
        out[place[i]] = total.astype(out.dtype)

    part = count // len(copies)
    for g, copy in enumerate(copies):
        copy.wait()
        in_steps(part, 8, lambda i, g=g: one(g * part + i))


IN_SMEM = pl.BlockSpec(memory_space=pltpu.SMEM)
IN_VMEM = pl.BlockSpec(memory_space=pltpu.VMEM)
IN_HBM = pl.BlockSpec(memory_space=pltpu.HBM)
PARAMS = pltpu.CompilerParams(vmem_limit_bytes=48 * 2**20)


def cost(field, tiles):
    return pl.CostEstimate(
        flops=16 * tiles.size * field.shape[1], bytes_accessed=2 * tiles.size, transcendentals=0
    )


def first_col_product(lists, field, tiles, out_tiles):
    count = lists[2].shape[0]
    slots, tile_size = tiles.shape[:2]
    blocks = (count, slots // count * tile_size, tile_size)
    return pl.pallas_call(
        functools.partial(first_col_kernel, slots // count),
        out_shape=(
            jax.ShapeDtypeStruct((out_tiles,) + field.shape[1:], jnp.float32),
            jax.ShapeDtypeStruct(blocks, tiles.dtype),
        ),
        in_specs=[IN_SMEM] * 3 + [IN_VMEM, IN_HBM],
        out_specs=(IN_VMEM, IN_HBM),
        scratch_shapes=[
            pltpu.VMEM(tiles.shape, tiles.dtype),
            pltpu.VMEM(blocks, tiles.dtype),
            pltpu.SemaphoreType.DMA((parts_of(slots, 8),)),
            pltpu.SemaphoreType.DMA((parts_of(count, 6),)),
        ],
        compiler_params=PARAMS,
        cost_estimate=cost(field, tiles),
    )(*lists, field, tiles)


def first_row_product(col_of, lists, field, tiles, out_tiles, tasks):
    count = lists[2].shape[0]
    slots, tile_size = tiles.shape[:2]
    blocks = (count, slots // count * tile_size, tile_size)
    return pl.pallas_call(
        functools.partial(first_row_kernel, slots // count),
        out_shape=(
            jax.ShapeDtypeStruct((out_tiles, tasks, tile_size), field.dtype),
            jax.ShapeDtypeStruct((out_tiles, 8, tile_size), jnp.float32),
            jax.ShapeDtypeStruct((field.shape[0], 8, tile_size), jnp.float32),
            jax.ShapeDtypeStruct(blocks, tiles.dtype),
        ),
        in_specs=[IN_SMEM] * 4 + [IN_VMEM, IN_HBM],
        out_specs=(IN_VMEM, IN_VMEM, IN_VMEM, IN_HBM),
        scratch_shapes=[
            pltpu.VMEM(tiles.shape, tiles.dtype),
            pltpu.VMEM(blocks, tiles.dtype),
            pltpu.SemaphoreType.DMA((parts_of(slots, 8),)),
            pltpu.SemaphoreType.DMA((parts_of(count, 12),)),
        ],
        compiler_params=PARAMS,
        cost_estimate=cost(field, tiles),
    )(col_of, *lists, field, tiles)


def next_product(lists, field, blocks, out_tiles, dtype):
    return pl.pallas_call(
        functools.partial(next_kernel, blocks.shape[1] // blocks.shape[2]),
        out_shape=jax.ShapeDtypeStruct((out_tiles,) + field.shape[1:], dtype),
        in_specs=[IN_SMEM] * 2 + [IN_VMEM, IN_HBM],
        out_specs=IN_VMEM,
        scratch_shapes=[
            pltpu.VMEM(blocks.shape, blocks.dtype),
            pltpu.SemaphoreType.DMA((parts_of(blocks.shape[0], 6),)),
        ],
        compiler_params=PARAMS,
        cost_estimate=cost(field, blocks),
    )(*lists[1:], field, blocks)


def lists_kernel(own_tiles, row_per, col_per, empty, here, row_source, col_source, *rest):
    by_row, by_row_loads, by_col, by_col_loads, col_of, ids, row_ids, col_ids, semaphores = rest
    copies = [
        pltpu.make_async_copy(row_source, row_ids, semaphores.at[0]),
        pltpu.make_async_copy(col_source, col_ids, semaphores.at[1]),
    ]
    for copy in copies:
        copy.start()
    for copy in copies:
        copy.wait()
    slots = row_ids.shape[1]
    size = ids.shape[1]
    lane = lax.broadcasted_iota(jnp.int32, (1, slots), 1)

    def parts(ids):
        piece = ((ids.astype(jnp.float32) + 0.5) * (1.0 / own_tiles)).astype(jnp.int32)
        return piece, ids - piece * own_tiles

    rows, cols = row_ids[...], col_ids[...]
    piece, inside = parts(rows)
    distance = piece ^ here[0]
    place = sum(
        jnp.where(distance == k, here[3 + k], 0) for k in range(here.shape[0] - 3)
    )
    row_loads = jnp.where(lane < here[2], place * own_tiles + inside, empty[0])
    piece, inside = parts(cols)
    col_loads = jnp.where(lane < here[2], (piece ^ here[1]) * own_tiles + inside, empty[1])
    ids[...] = jnp.full(ids.shape, size, jnp.int32)
    for k, values in enumerate((rows, cols, col_loads, row_loads)):
        ids[k : k + 1, :slots] = values
    across = ids[...]
    col_of[...] = across[2:3]
    down = across.T
    first = lax.broadcasted_iota(jnp.int32, (size, size), 0)
    second = lax.broadcasted_iota(jnp.int32, (size, size), 1)
    for k, per, order, loads in (
        (0, row_per, by_row, by_row_loads),
        (1, col_per, by_col, by_col_loads),
    ):
        key = down[:, k : k + 1]
        before = (key == across[k : k + 1]) & (second < first)
        rank = jnp.sum(before.astype(jnp.float32), axis=1, keepdims=True).astype(jnp.int32)
        chosen = key * per + rank == second
        order[...] = jnp.sum(jnp.where(chosen, first, 0), axis=0, keepdims=True)
        loads[...] = jnp.sum(jnp.where(chosen, down[:, 2 + k : 3 + k], 0), axis=0, keepdims=True)


def sorted_lists(own_tiles, row_per, col_per, empty, here, row_ids, col_ids):
    size = -(-row_ids.shape[1] // 128) * 128
    return pl.pallas_call(
        functools.partial(lists_kernel, own_tiles, row_per, col_per, empty),
        out_shape=[jax.ShapeDtypeStruct((1, size), jnp.int32)] * 5,
        in_specs=[IN_SMEM, IN_HBM, IN_HBM],
        out_specs=[IN_VMEM] * 5,
        scratch_shapes=[
            pltpu.VMEM((8, size), jnp.int32),
            pltpu.VMEM(row_ids.shape, jnp.int32),
            pltpu.VMEM(row_ids.shape, jnp.int32),
            pltpu.SemaphoreType.DMA((2,)),
        ],
        compiler_params=PARAMS,
    )(here, row_ids, col_ids)


def addends(value, count):
    parts = []
    for _ in range(count):
        high = lax.reduce_precision(value, 8, 7)
        parts.append(high)
        value = value - high
    return jnp.stack(parts).astype(jnp.bfloat16)


def join(parts):
    return jnp.sum(parts.astype(jnp.float32), axis=0)


def rows_to_tiles(rows, tile_rows):
    count = -(-rows.shape[0] // tile_rows)
    rows = jnp.pad(rows, ((0, count * tile_rows - rows.shape[0]), (0, 0)))
    return rows.reshape(count, tile_rows, rows.shape[1])


def tiles_to_rows(tiles, count):
    return tiles.reshape(-1, tiles.shape[2])[:count]


class Plan:
    def __init__(self, rows, cols):
        self.rows, self.cols = rows, cols
        self.row_steps = [("row", m) for m in range(1, rows // 2)]
        first = self.row_steps + [("col", k) for k in range(cols - 2, 0, -2)]
        second = [("col", k) for k in range(cols - 1, 0, -2)]
        while len(first) > len(second) + 1:
            second.append(first.pop())
        first += [None] * (len(second) - len(first))
        second += [None] * (len(first) - len(second))
        self.count = len(first)
        self.steps = list(zip(first, second, strict=True))
        self.sum_steps = [(None if a in self.row_steps else a, b) for a, b in self.steps]
        place = np.zeros((2, cols), np.int32)
        for j, pair in enumerate(self.steps):
            for core, partner in enumerate(pair):
                if partner is not None and partner[0] == "col":
                    place[core, partner[1]] = 1 + j
                    place[1 - core, partner[1]] = 1 + self.count + j
        self.place = place

    def pairs(self, by_core):
        found = []
        for r in range(self.rows):
            partner = by_core[r % 2]
            if partner is None:
                continue
            axis, k = partner
            for c in range(self.cols):
                to = (r ^ (2 * k), c) if axis == "row" else (r, c ^ k)
                found.append((r * self.cols + c, to[0] * self.cols + to[1]))
        return found

    def send(self, value, by_core):
        return lax.ppermute(value, MESH_AXES, self.pairs(by_core))

    def swap(self, value):
        return lax.ppermute(value, "row", [(r, r ^ 1) for r in range(self.rows)])


def per_device(plan, scores, tile_values, tile_rows, tile_cols, tile_count):
    tiles = tile_values[0, 0]
    row_ids = tile_rows[0]
    col_ids = tile_cols[0]
    live = tile_count[0, 0]
    slots, tile_size = tiles.shape[:2]
    task_count, piece_len = scores.shape
    own_tiles = piece_len // tile_size
    row_tiles, col_tiles = own_tiles * plan.cols, own_tiles * plan.rows
    low_part = own_tiles * plan.count
    row_pieces = own_tiles + 2 * low_part
    row_index, col_index = lax.axis_index("row"), lax.axis_index("col")
    core = row_index % 2
    low = jnp.bfloat16

    place_of = jnp.where(core == 0, jnp.asarray(plan.place[0]), jnp.asarray(plan.place[1]))

    def row_place(ids):
        piece = (ids // own_tiles) ^ col_index
        chosen = piece[:, None] == jnp.arange(plan.cols, dtype=jnp.int32)[None, :]
        piece = jnp.sum(jnp.where(chosen, place_of[None, :], 0), axis=1, dtype=jnp.int32)
        return piece * own_tiles + ids % own_tiles

    def col_place(ids):
        return ((ids // own_tiles) ^ row_index) * own_tiles + ids % own_tiles

    def make_lists(row_ids, col_ids, live):
        here = jnp.concatenate([jnp.stack([col_index, row_index, live]), place_of])
        by_row, by_row_loads, by_col, by_col_loads, col_of = sorted_lists(
            own_tiles, slots // row_tiles, slots // col_tiles, (row_pieces, col_tiles), here,
            row_ids, col_ids,
        )
        by_row = [by_row, by_row_loads, row_place(jnp.arange(row_tiles, dtype=jnp.int32))]
        by_col = [by_col, by_col_loads, col_place(jnp.arange(col_tiles, dtype=jnp.int32))]
        return col_of, by_row, by_col

    def empty_tile(field):
        return jnp.zeros((1,) + field.shape[1:], field.dtype)

    def with_ones(field):
        field = jnp.pad(field[:-1], ((0, 0), (0, 16), (0, 0)), constant_values=1)
        return jnp.pad(field, ((0, 1), (0, 0), (0, 0)))

    def pack(degree):
        return rows_to_tiles(addends(degree, 2).reshape(-1, tile_size), task_count)

    def unpack(tiles, count):
        return join(tiles_to_rows(tiles, 2 * count).reshape(2, count, tile_size))

    def pack_dots(dots):
        parts = addends(dots, 2)
        return (parts[0] + jnp.pad(parts[1, :, :-DOTS], ((0, 0), (DOTS, 0))))[None]

    def unpack_dots(tile):
        tile = tile.astype(jnp.float32)
        tile = tile + jnp.pad(tile[:, DOTS:], ((0, 0), (0, DOTS)))
        return jnp.where(lax.broadcasted_iota(jnp.int32, tile.shape, 1) < DOTS, tile, 0.0)

    def inner(a, b):
        return jnp.sum(a.astype(jnp.float32) * b.astype(jnp.float32), axis=(0, 2))[:, None]

    def as_tile(columns):
        at = lax.broadcasted_iota(jnp.int32, (task_count, tile_size), 1)
        return sum(jnp.where(at == i, column, 0.0) for i, column in enumerate(columns))

    near = len(plan.row_steps)
    chip_rows = plan.rows // 2
    chip = 2 * own_tiles
    own = slice(0, own_tiles)
    residual = scores.reshape(task_count, own_tiles, tile_size).transpose(1, 0, 2)
    residual = jnp.concatenate([residual, plan.swap(residual)])
    solution = direction = image = None
    norm_before = curve_before = scale = None
    for step_index in range(ITERS):
        first = step_index == 0

        pair = residual.astype(low)
        if first:
            pair, row_ids, col_ids, live = lax.optimization_barrier((pair, row_ids, col_ids, live))
            col_of, by_row, by_col = make_lists(row_ids, col_ids, live)
        got = [plan.send(pair, by_core) for by_core in plan.steps]
        if first:
            nearby, by_row = lax.optimization_barrier((got[:near], by_row))
            got = nearby + got[near:]
        shared = [plan.swap(g) for g in got[:near]]
        col_pieces = [pair]
        for g, other in zip(got, shared):
            col_pieces.append(jnp.where(core == 0, g[:own_tiles], other[own_tiles:]))
            col_pieces.append(jnp.where(core == 0, g[own_tiles:], other[:own_tiles]))
        col_field = jnp.concatenate(col_pieces + [empty_tile(pair)])
        if first:
            forward, row_degree, col_degree, row_blocks = first_row_product(
                col_of, by_row, with_ones(col_field), tiles, row_pieces, task_count
            )
        else:
            forward = next_product(by_row, col_field, row_blocks, row_pieces, low)

        far, forward = lax.optimization_barrier((got[near:], forward))
        mine = [g[:own_tiles] for g in got[:near] + far]
        swapped = plan.swap(jnp.concatenate([g[own_tiles:] for g in far]))
        row_field = jnp.concatenate(
            [pair[own]] + mine + [o[own_tiles:] for o in shared] + [swapped, empty_tile(pair)]
        )
        curve_part = -inner(row_field[:-1], forward)
        norm = inner(residual[own], residual[own])
        if first:
            row_degree = row_degree[:, 0]
            weights = 0.5 * coupling * row_degree[:, None]
            curve_part = coupling * curve_part
            curve_part += inner(row_field[:-1].astype(jnp.float32) ** 2, weights)
            col_degree = jnp.sum(col_degree[:-1], axis=1)
            weights = 0.5 * coupling * col_degree[:, None]
            curve_part += inner(col_field[:-1].astype(jnp.float32) ** 2, weights)
            dots = as_tile([norm, norm + curve_part])
        else:
            weighted = inner(scale[own] * residual[own], residual[own])
            along = inner(residual[own], image[own])
            dots = as_tile([norm, weighted + coupling * curve_part, along])

        parts = [forward[own_tiles + low_part :], pack_dots(dots)]
        if first:
            col_degree = col_degree.reshape(chip_rows, chip, tile_size)
            parts.append(pack(row_degree[own_tiles + low_part :]))
        swapped = plan.swap(jnp.concatenate(parts))
        swapped, row_field = lax.optimization_barrier((swapped, row_field))
        if first:
            other_degree = unpack(swapped[low_part + 1 :], low_part)
        if first:
            backward, col_blocks = first_col_product(by_col, row_field, tiles, col_tiles)
        else:
            backward = next_product(by_col, row_field, col_blocks, col_tiles, jnp.float32)
        dots = dots + unpack_dots(swapped[low_part])
        dots_low = pack_dots(dots)
        mine_products = forward[own]
        messages = []
        order = list(range(plan.count))
        for j in order[1:] + order[:1]:
            by_core = plan.sum_steps[j]
            piece = slice(j * own_tiles, (j + 1) * own_tiles)
            message = [forward[own_tiles:][piece], swapped[:low_part][piece], dots_low]
            if first:
                degrees = [row_degree[own_tiles:][piece], other_degree[piece]]
                message.append(pack(jnp.concatenate(degrees)))
            messages.append(plan.send(jnp.concatenate(message), by_core))

        backward = backward.reshape(chip_rows, chip, task_count, tile_size)
        returned = []
        for m, by_core in enumerate(plan.row_steps, 1):
            returned.append(plan.send(backward[m].astype(low), (by_core,) * 2))
        total = sum(m.astype(jnp.float32) for m in messages)
        dots = jnp.where(core == 0, dots, 0.0) + unpack_dots(total[chip])
        dots_mine = dots
        degree_back = col_degree[0] if first else None
        for m, by_core in enumerate(plan.row_steps, 1):
            message = jnp.concatenate([dots_mine, col_degree[m]]) if first else dots_mine
            back = plan.send(message, (by_core,) * 2)
            dots = dots + back[:task_count]
            if first:
                degree_back = degree_back + back[task_count:]
        if first:
            degree = unpack(total[chip + 1 :], chip) + degree_back
            degree += jnp.pad(row_degree[own], ((0, own_tiles), (0, 0)))
        total = total[:chip] + backward[0]
        total += jnp.pad(mine_products.astype(jnp.float32), ((0, own_tiles), (0, 0), (0, 0)))
        total += sum(back.astype(jnp.float32) for back in returned)

        message = [total, dots[None]]
        if first:
            message.append(rows_to_tiles(degree, task_count))
        back = plan.swap(jnp.concatenate(message))
        total = 0.5 * (total + jnp.concatenate([back[own_tiles:chip], back[own]]))
        dots = dots + back[chip]
        if first:
            back = tiles_to_rows(back[chip + 1 :], chip)
            degree = degree + jnp.concatenate([back[own_tiles:], back[own]])

        norm, curve, along = dots[:, 0:1], dots[:, 1:2], dots[:, 2:3]
        if first:
            scale = 1.0 + 0.5 * coupling * degree[:, None]
        fresh = scale * residual - coupling * total
        if first:
            direction, image = residual, fresh
        else:
            ratio = norm / norm_before
            curve = curve + 2.0 * ratio * along + ratio * ratio * curve_before
            direction = residual + ratio * direction
            image = fresh + ratio * image
        norm_before, curve_before = norm, curve
        step_size = norm / curve
        solution = step_size * direction if first else solution + step_size * direction
        residual = residual - step_size * image

    return tuple(to_fields(solution[own], residual[own]))


def solution(mesh):
    plan = Plan(mesh.shape["row"], mesh.shape["col"])
    return jax.shard_map(
        functools.partial(per_device, plan),
        mesh=mesh,
        in_specs=(
            P(None, ("row", "col")),
            P("row", "col", None, None, None),
            P("row", "col", None),
            P("row", "col", None),
            P("row", "col"),
        ),
        out_specs=(P(None, ("row", "col")), P(None, ("row", "col"))),
        check_vma=False,
    )
```
